1024 devices in a mesh: section: 2 (over y_lo), tensor: 8 (over y_hi, x), dp: 64 (over z, core).
Axes of the slice: x: 4, y: 4 (y_hi: 2, y_lo: 2; y = y_hi * 2 + y_lo), z: 32, core: 2. Of those that a mesh axis runs over, the one named last changes fastest.
Arguments:
- cotangent: bfloat16 [2, 64, 128, 2048], P('section', 'dp', 'tensor'), may hold values from -6 to 6
- saved_input: bfloat16 [2, 2, 2, 64, 128, 2048], P(None, 'section', None, 'dp', 'tensor'), may hold values from -6 to 6
- saved_normed: bfloat16 [2, 2, 2, 64, 128, 2048], P(None, 'section', None, 'dp'), may hold values from -16 to 16
- saved_query: bfloat16 [2, 2, 2, 64, 128, 2048], P(None, 'section', None, 'dp', None, 'tensor'), may hold values from -6 to 6
- saved_keyval: bfloat16 [2, 2, 2, 64, 128, 8, 128], P(None, 'section', None, 'dp', None, 'tensor'), may hold values from -6 to 6
- norm_gain: float32 [2, 2, 2048], P(None, 'section'), may hold values from 0.5 to 1.5
- w_query: bfloat16 [2, 2, 2048, 2048], P(None, 'section', None, 'tensor'), may hold values from -0.125 to 0.125
- w_keyval: bfloat16 [2, 2, 2048, 8, 128], P(None, 'section', None, 'tensor'), may hold values from -0.125 to 0.125
- w_output: bfloat16 [2, 2, 2048, 2048], P(None, 'section', 'tensor'), may hold values from -0.125 to 0.125
Outputs:
- input_grad: bfloat16 [2, 64, 128, 2048], P('section', 'dp', 'tensor')
- keyval_grad: float32 [2, 2, 2048, 8, 128], P(None, 'section', 'dp', 'tensor')
The draws below stay inside these ranges and needn't reach their ends.
All inputs are finite; a program needn't handle non-finite values.
Results may differ from the reference program's by a relative error of at most 0.035.
Values may be sent and summed in bfloat16 or wider, within the bound.
A program may use at most 64 MiB of HBM per device.

```python
import jax
import jax.numpy as jnp
from jax import lax

D = 2048
HEADS = 32
KV = 8
HD = 64
SEQ = 128
LAYERS_DEV = 2
SECTIONS = 2
MICRO = 2
SEQS = 64
N_SECTION = 2
N_TENSOR = 8


def spiked(array, key, source, target, shards_of, factor):
    def block_of(position):
        return (jnp.arange(array.shape[position]) // (array.shape[position] // shards_of)).reshape((-1,) + (1,) * (array.ndim - 1 - position))

    first = jax.random.permutation(key, shards_of)[block_of(target)]
    other_side = (block_of(target) + shards_of // 2) % shards_of
    return jnp.where((block_of(source) == first) | (block_of(source) == other_side), factor * array, array)


def steps_of(stream_key, extent, cuts, least, high):
    loudness, own = 1.0, jax.random.fold_in(stream_key, 6)
    for position, blocks in cuts:
        draws = jnp.exp(jax.random.uniform(jax.random.fold_in(own, position), (blocks,), jnp.float32, least / len(cuts), high / len(cuts)))
        loudness = loudness * jnp.repeat(draws, extent[position] // blocks).reshape([-1 if axis == position else 1 for axis in range(len(extent))])
    return loudness


def centred(key, extent, deviation, bound, cuts=(), dtype=jnp.bfloat16):
    factor_of = steps_of(key, extent, cuts, -0.22, 0.18) if cuts else 1.0
    entries = jax.random.normal(key, extent, jnp.float32) * deviation * factor_of
    return jnp.minimum(jnp.maximum(entries, -bound), bound).astype(dtype)


def gaussian_with(stream_key, dims, scale, most, cuts, heavy, kind=jnp.bfloat16):
    result = scale * jax.random.normal(stream_key, dims, jnp.float32)
    if cuts:
        result = result * steps_of(stream_key, dims, cuts, -0.22, 0.18)
    return jnp.clip(spiked(result, jax.random.fold_in(stream_key, 3), *heavy), -most, most).astype(kind)


def setup_inputs(seed: int = 0) -> dict:
    seeds = jax.random.split(jax.random.key(seed), 10)
    cotangent = centred(seeds[0], (MICRO, SEQS, SEQ, D), 1.0, 6.0, ((0, 2), (1, 64), (2, 8)))
    saved_input = centred(seeds[1], (LAYERS_DEV, SECTIONS, MICRO, SEQS, SEQ, D), 1.0, 6.0, ((1, 2), (3, 64), (4, 8)))
    saved_normed = gaussian_with(seeds[2], (LAYERS_DEV, SECTIONS, MICRO, SEQS, SEQ, D), 1.0, 16.0, ((1, 2), (3, 64)), (3, 5, 64, 4.0))
    saved_query = centred(seeds[3], (LAYERS_DEV, SECTIONS, MICRO, SEQS, SEQ, HEADS * HD), 1.0, 6.0, ((1, 2), (3, 64), (5, 8)))
    saved_keyval = centred(seeds[4], (LAYERS_DEV, SECTIONS, MICRO, SEQS, SEQ, KV, 2 * HD), 1.0, 6.0, ((1, 2), (3, 64), (5, 8)))
    norm_gain = jnp.clip(1.0 + 0.1 * jax.random.normal(seeds[5], (LAYERS_DEV, SECTIONS, D), jnp.float32), 0.5, 1.5)
    w_query = centred(seeds[6], (LAYERS_DEV, SECTIONS, D, HEADS * HD), D ** -0.5, 0.125, ((1, 2), (3, 8)))
    w_keyval = centred(seeds[7], (LAYERS_DEV, SECTIONS, D, KV, 2 * HD), D ** -0.5, 0.125, ((1, 2), (3, 8)))
    w_output = centred(seeds[8], (LAYERS_DEV, SECTIONS, HEADS * HD, D), (HEADS * HD) ** -0.5, 0.125, ((1, 2), (2, 8)))
    return dict(cotangent=cotangent, saved_input=saved_input, saved_normed=saved_normed, saved_query=saved_query, saved_keyval=saved_keyval, norm_gain=norm_gain, w_query=w_query, w_keyval=w_keyval, w_output=w_output)


def attend(query, keyval):
    n_batch, n_rows, query_width = query.shape
    kv_heads = keyval.shape[2]
    head_size = keyval.shape[3] // 2
    groups = query_width // (kv_heads * head_size)
    query_f = query.astype(jnp.float32).reshape(n_batch, n_rows, kv_heads, groups, head_size)
    key_rows = keyval[..., :head_size].astype(jnp.float32)
    values = keyval[..., head_size:].astype(jnp.float32)
    scores = jnp.einsum('bqhgd,bkhd->bhgqk', query_f, key_rows) * head_size ** (-0.5)
    places = jnp.arange(n_rows)
    causal = places[:, None] >= places[None, :]
    scores = jnp.where(causal, scores, -1e+30)
    highest = lax.stop_gradient(lax.optimization_barrier(jnp.max(scores, axis=-1, keepdims=True)))
    weights = jnp.exp(scores - highest)
    shares = (weights / lax.optimization_barrier(jnp.sum(weights, axis=-1, keepdims=True))).astype(jnp.bfloat16)
    mixture = jnp.einsum('bhgqk,bkhd->bqhgd', shares.astype(jnp.float32), values)
    return mixture.reshape(n_batch, n_rows, query_width).astype(jnp.bfloat16)

def normalize(values, gain_row):
    mean_sq = lax.optimization_barrier(jnp.mean(values * values, axis=-1, keepdims=True))
    return values * lax.rsqrt(mean_sq + 1e-05) * gain_row

def reference(cotangent, saved_input, saved_normed, saved_query, saved_keyval, norm_gain, w_query, w_keyval, w_output):
    batch_rows = MICRO * SEQS
    query_width = HEADS // N_TENSOR * HD
    kv_heads = KV // N_TENSOR
    kv_span = kv_heads * 2 * HD
    upstream = cotangent.reshape(batch_rows, SEQ, D)
    grad_table = {}
    for layer in reversed(range(LAYERS_DEV * N_SECTION)):
        slot, place = (layer // N_SECTION, layer % N_SECTION)
        inputs_x = saved_input[slot, place].reshape(batch_rows, SEQ, D)
        normed = saved_normed[slot, place].reshape(batch_rows, SEQ, D).astype(jnp.float32)
        query_all = saved_query[slot, place].reshape(batch_rows, SEQ, HEADS * HD)
        keyval_all = saved_keyval[slot, place].reshape(batch_rows, SEQ, KV, 2 * HD)
        upstream_f = upstream.astype(jnp.float32)
        d_normed = jnp.zeros((batch_rows, SEQ, D), jnp.float32)
        pieces = []
        for group in range(N_TENSOR):
            qs = slice(group * query_width, (group + 1) * query_width)
            ks = slice(group * kv_heads, (group + 1) * kv_heads)
            w_out = w_output[slot, place][qs].astype(jnp.float32)
            d_attn = jnp.einsum('bsd,ad->bsa', upstream_f, w_out).astype(jnp.bfloat16)
            _, pull = jax.vjp(attend, query_all[..., qs], keyval_all[:, :, ks])
            d_query, d_keyval = pull(d_attn)
            d_kv_flat = d_keyval.reshape(batch_rows, SEQ, kv_span).astype(jnp.float32)
            w_q = w_query[slot, place][:, qs].astype(jnp.float32)
            w_kv = w_keyval[slot, place][:, ks].reshape(D, kv_span).astype(jnp.float32)
            part = jnp.einsum('bsa,da->bsd', d_query.astype(jnp.float32), w_q)
            part = part + jnp.einsum('bsk,dk->bsd', d_kv_flat, w_kv)
            d_normed = d_normed + lax.optimization_barrier(part.astype(jnp.bfloat16)).astype(jnp.float32)
            pieces.append(jnp.einsum('bsd,bsk->dk', normed, d_kv_flat).reshape(D, kv_heads, 2 * HD))
        grad_table[slot, place] = jnp.concatenate(pieces, axis=1)
        gain_row = norm_gain[slot, place]
        _, pull_norm = jax.vjp(lambda values: normalize(values, gain_row), inputs_x.astype(jnp.float32))
        d_input = pull_norm(d_normed)[0]
        upstream = (upstream_f + d_input).astype(jnp.bfloat16)
    keyval_grad = jnp.stack([jnp.stack([grad_table[slot, place] for place in range(N_SECTION)]) for slot in range(LAYERS_DEV)])
    return (upstream.reshape(MICRO, SEQS, SEQ, D), keyval_grad)
```

```python
import functools

import jax
import jax.numpy as jnp
from jax import lax
from jax.experimental import pallas as pl
from jax.experimental.pallas import tpu as pltpu
from jax.sharding import PartitionSpec as P

MESH = pl.DeviceIdType.MESH
BF16 = jnp.bfloat16
F32 = jnp.float32
NT = (((1,), (1,)), ((), ()))
TN = (((0,), (0,)), ((), ()))
NN = (((1,), (0,)), ((), ()))
NEAR = 4


def dot(a, b, dims):
    return lax.dot_general(a, b, dims, preferred_element_type=F32)


def attention_grads(query, keyval, d_attn):
    rows, q_width = query.shape
    head = keyval.shape[1] // 2
    n_heads = q_width // head
    scale = head**-0.5
    low = lax.broadcasted_iota(jnp.int32, (rows, 2 * head), 1) < head
    kv = keyval.astype(F32)
    vk = pltpu.roll(kv, head, 1)
    zero = jnp.zeros((rows, 2 * head), BF16)
    k_low = jnp.where(low, kv * scale, 0.0).astype(BF16)
    k_high = jnp.where(low, 0.0, vk * scale).astype(BF16)
    v_low = jnp.where(low, vk, 0.0).astype(BF16)
    v_high = jnp.where(low, 0.0, kv).astype(BF16)

    def spread(even, odd):
        parts = []
        for i in range(n_heads):
            own = odd if i % 2 else even
            parts.append(
                jnp.concatenate(
                    [own if i // 2 == p else zero for p in range(n_heads // 2)], axis=1
                )
            )
        return jnp.concatenate(parts, axis=0)

    keys = spread(k_low, k_high)
    values = spread(v_low, v_high)
    scores = dot(keys, query, NT)
    d_share = dot(values, d_attn, NT)
    causal = lax.broadcasted_iota(jnp.int32, (rows, rows), 0) <= lax.broadcasted_iota(
        jnp.int32, (rows, rows), 1
    )
    shares, d_scores = [], []
    for i in range(n_heads):
        s = jnp.where(causal, scores[i * rows : (i + 1) * rows], -1e30)
        e = jnp.exp(s - jnp.max(s, axis=0, keepdims=True))
        p = e / jnp.sum(e, axis=0, keepdims=True)
        dp = d_share[i * rows : (i + 1) * rows]
        ds = p * (dp - jnp.sum(p * dp, axis=0, keepdims=True))
        shares.append(p.astype(BF16))
        d_scores.append(ds.astype(BF16))
    d_query = dot(jnp.concatenate(d_scores, axis=0), keys, TN)

    def by_parity(blocks):
        return jnp.concatenate(
            [jnp.concatenate(blocks[0::2], axis=1), jnp.concatenate(blocks[1::2], axis=1)], axis=0
        )

    def stacked(array):
        return jnp.concatenate(
            [array[:, p * 2 * head : (p + 1) * 2 * head] for p in range(n_heads // 2)], axis=0
        )

    dk = dot(by_parity(d_scores), stacked(query), NN) * scale
    dv = dot(by_parity(shares), stacked(d_attn), NN)
    d_keyval = jnp.where(low, dk[:rows], dv[rows:]) + pltpu.roll(
        jnp.where(low, dv[:rows], dk[rows:]), head, 1
    )
    return d_query.astype(BF16), d_keyval.astype(BF16)


def kernel(
    n_tensor,
    n_dp,
    cot_hbm,
    xin_hbm,
    xn_hbm,
    q_hbm,
    kv_hbm,
    gain_hbm,
    wq_hbm,
    wkv_hbm,
    wo_hbm,
    out_ref,
    grad_ref,
    xin,
    xn,
    q,
    kv,
    gain,
    wq,
    wkv,
    wo,
    gathered,
    parts,
    landed,
    outs,
    final,
    dkv,
    turned,
    core_out,
    core_own,
    core_in,
    z1_out,
    z1_in,
    z2_out,
    z2_in,
    load_sem,
    ag_send,
    ag_recv,
    out_send,
    rs_send,
    rs_recv,
    fin_send,
    fin_recv,
    core_send,
    core_recv,
    z1_send,
    z1_recv,
    z2_send,
    z2_recv,
    go_sem,
    token_sem,
):
    s = lax.axis_index("section")
    t = lax.axis_index("tensor")
    d = lax.axis_index("dp")
    z, core = d // 2, d % 2
    n_z = n_dp // 2
    n_far = n_z // NEAR
    zi, zg = z % NEAR, z // NEAR
    shard = outs.shape[1]
    n_rows = q.shape[2]
    chunk = grad_ref.shape[1]
    first = s == 1

    def tensor_peer(j):
        return lax.rem(t + j, n_tensor)

    def near_peer(j):
        return (zg * NEAR + lax.rem(zi + j, NEAR)) * 2 + core

    def far_peer(j):
        return (lax.rem(zg + j, n_far) * NEAR + zi) * 2 + core

    barrier = pltpu.get_barrier_semaphore()

    def hello(device):
        pl.semaphore_signal(barrier, inc=1, device_id=device, device_id_type=MESH)

    for j in range(1, n_tensor):
        hello({"tensor": tensor_peer(j)})
    for j in range(n_tensor):
        hello({"section": 1 - s, "tensor": tensor_peer(j)})
    hello({"dp": z * 2 + 1 - core})
    for j in range(1, NEAR):
        hello({"dp": near_peer(j)})
    for j in (1, n_far - 1):
        hello({"dp": far_peer(j)})

    loads = [
        pltpu.make_async_copy(src, dst, load_sem.at[i])
        for i, (src, dst) in enumerate(
            [
                (wo_hbm, wo),
                (q_hbm, q),
                (kv_hbm, kv),
                (wq_hbm, wq),
                (wkv_hbm, wkv),
                (xin_hbm, xin),
                (gain_hbm, gain),
                (xn_hbm, xn),
            ]
        )
    ]
    for load in loads:
        load.start()

    pl.semaphore_wait(barrier, 2 * n_tensor - 1 + 1 + NEAR - 1 + 2)

    def rows_of(index):
        return pl.ds(pl.multiple_of(index * shard, shard), shard)

    def gather_copy(src, item, j, section):
        return pltpu.make_async_remote_copy(
            src_ref=src,
            dst_ref=gathered.at[item, rows_of(t)],
            send_sem=ag_send.at[item, j],
            recv_sem=ag_recv.at[item, j],
            device_id={"section": section, "tensor": tensor_peer(j)},
            device_id_type=MESH,
        )

    def reply_copy(k, item, j):
        return pltpu.make_async_remote_copy(
            src_ref=outs.at[k],
            dst_ref=gathered.at[item, rows_of(t)],
            send_sem=out_send.at[k, j],
            recv_sem=ag_recv.at[item, j],
            device_id={"section": 1 - s, "tensor": tensor_peer(j)},
            device_id_type=MESH,
        )

    def own_shard_copy():
        return pltpu.make_async_copy(cot_hbm, gathered.at[0, rows_of(t)], ag_recv.at[0, 0])

    def reduce_copy(k, j):
        return pltpu.make_async_remote_copy(
            src_ref=parts.at[k, rows_of(tensor_peer(j))],
            dst_ref=landed.at[k, rows_of(j)],
            send_sem=rs_send.at[k, j],
            recv_sem=rs_recv.at[k, j],
            device_id={"tensor": tensor_peer(j)},
            device_id_type=MESH,
        )

    def final_copy():
        return pltpu.make_async_remote_copy(
            src_ref=outs.at[2],
            dst_ref=final,
            send_sem=fin_send,
            recv_sem=fin_recv,
            device_id={"section": 1 - s},
            device_id_type=MESH,
        )

    def core_copy(slot):
        return pltpu.make_async_remote_copy(
            src_ref=core_out.at[slot],
            dst_ref=core_in.at[slot],
            send_sem=core_send.at[slot],
            recv_sem=core_recv.at[slot],
            device_id={"dp": z * 2 + 1 - core},
            device_id_type=MESH,
        )

    def near_copy(slot, j):
        return pltpu.make_async_remote_copy(
            src_ref=z1_out.at[slot, lax.rem(zi + j, NEAR)],
            dst_ref=z1_in.at[slot, j],
            send_sem=z1_send.at[slot, j],
            recv_sem=z1_recv.at[slot, j],
            device_id={"dp": near_peer(j)},
            device_id_type=MESH,
        )

    def far_copy(slot, j):
        return pltpu.make_async_remote_copy(
            src_ref=z2_out.at[slot, lax.rem(zg + j, n_far)],
            dst_ref=z2_in.at[slot, j],
            send_sem=z2_send.at[slot, j],
            recv_sem=z2_recv.at[slot, j],
            device_id={"dp": far_peer(j)},
            device_id_type=MESH,
        )

    def greet(round_index):
        for j in (1, n_far - 1):
            pl.semaphore_signal(
                token_sem.at[round_index],
                inc=1,
                device_id={"dp": far_peer(j)},
                device_id_type=MESH,
            )

    def greeted(round_index):
        pl.semaphore_wait(token_sem.at[round_index], 2)

    def turn(slot):
        def block(b, carry):
            columns = pl.ds(pl.multiple_of(b * 128, 128), 128)
            for place in range(2):
                flat = xn[slot, 1 - place, :, columns].T
                for i in range(128 // chunk):
                    owner = b * (128 // chunk) + i
                    oz, oc = owner // 2, owner % 2
                    where = (oz % NEAR) * n_far + oz // NEAR
                    turned[
                        slot,
                        oc,
                        pl.ds(pl.multiple_of(where * chunk, chunk), chunk),
                        place * n_rows : (place + 1) * n_rows,
                    ] = flat[i * chunk : (i + 1) * chunk]
            return carry

        lax.fori_loop(0, xn.shape[3] // 128, block, 0)

    def gradient(slot):
        rows = dkv[slot]

        def theirs(b, carry):
            span = pl.ds(pl.multiple_of(b * 256, 256), 256)
            core_out[slot, span] = dot(turned[slot, 1 - core, span], rows, NN).astype(BF16)
            return carry

        def ours(b, carry):
            span = pl.ds(pl.multiple_of(b * 256, 256), 256)
            core_own[slot, span] = dot(turned[slot, core, span], rows, NN)
            return carry

        count = core_out.shape[1] // 256
        lax.fori_loop(0, count, theirs, 0)
        core_copy(slot).start()
        lax.fori_loop(0, count, ours, 0)

    def near_phase(slot):
        core_copy(slot).wait_recv()
        block = n_far * chunk
        for i in range(NEAR):
            span = slice(i * block, (i + 1) * block)
            total = core_own[slot, span] + core_in[slot, span].astype(F32)
            core_own[slot, span] = total
            z1_out[slot, i] = total.astype(BF16)
        for j in range(1, NEAR):
            near_copy(slot, j).start()

    def far_phase(slot):
        block = n_far * chunk
        total = core_own[slot, pl.ds(pl.multiple_of(zi * block, block), block)]
        for j in range(1, NEAR):
            near_copy(slot, j).wait_recv()
            total = total + z1_in[slot, j].astype(F32)
        for g in range(n_far):
            piece = total[g * chunk : (g + 1) * chunk]
            z2_out[slot, g] = piece.astype(BF16)

            @pl.when(g == zg)
            def _():
                grad_ref[slot] = piece

        for j in range(1, n_far):
            far_copy(slot, j).start()

    def last_phase(slot):
        total = grad_ref[slot]
        for j in range(1, n_far):
            far_copy(slot, j).wait_recv()
            total = total + z2_in[slot, j].astype(F32)
        grad_ref[slot] = total

    @pl.when(first)
    def _():
        for j in range(1, n_tensor):
            gather_copy(cot_hbm, 0, j, s).start()
        own_shard_copy().start()

    greet(0)
    for load in loads:
        load.wait()

    @pl.when(jnp.logical_not(first))
    def _():
        pl.semaphore_wait(go_sem, 1)
        for j in range(n_tensor):
            gather_copy(cot_hbm, 1, j, 1 - s).start()

    def step(k, carry):
        slot = 1 - k // 2
        place = k % 2
        micro = 1 - place
        tail = jnp.logical_and(k == 3, jnp.logical_not(first))
        for j in range(n_tensor):
            gather_copy(outs.at[0], k, j, s).wait_recv()

        @pl.when(jnp.logical_and(first, k == 0))
        def _():
            pl.semaphore_signal(go_sem, inc=1, device_id={"section": 1 - s}, device_id_type=MESH)

        d_attn = dot(gathered[k], wo[slot], NT).astype(BF16)
        d_query, d_keyval = attention_grads(q[slot, micro], kv[slot, micro], d_attn)
        dkv[slot, pl.ds(pl.multiple_of(place * n_rows, n_rows), n_rows)] = d_keyval

        @pl.when(tail)
        def _():
            gradient(0)

        parts[k] = (dot(d_query, wq[slot], NT) + dot(d_keyval, wkv[slot], NT)).astype(BF16)

        @pl.when(tail)
        def _():
            near_phase(0)

        for j in range(1, n_tensor):
            reduce_copy(k, j).start()

        @pl.when(place == 0)
        def _():
            turn(slot)

        @pl.when(jnp.logical_and(place == 1, jnp.logical_not(tail)))
        def _():
            gradient(slot)
            near_phase(slot)

        @pl.when(k < 2)
        def _():
            greeted(k)
            greet(k + 1)

        @pl.when(k == 2)
        def _():
            greeted(2)
            far_phase(1)

        @pl.when(tail)
        def _():
            far_phase(0)

        x = xin[slot, micro].astype(F32)
        mean_sq = jnp.mean(x * x, axis=-1, keepdims=True)
        r = lax.rsqrt(mean_sq + 1e-05)
        d_normed = parts[k, rows_of(t)].astype(F32)
        for j in range(1, n_tensor):
            reduce_copy(k, j).wait_recv()
            d_normed = d_normed + landed[k, j * shard : (j + 1) * shard].astype(F32)
        scaled = d_normed * gain[slot]
        along = jnp.mean(x * scaled, axis=-1, keepdims=True)
        d_input = r * scaled - x * (r * r * r * along)
        outs[k] = (gathered[k, rows_of(t)].astype(F32) + d_input).astype(BF16)

        @pl.when(first)
        def _():
            for j in range(n_tensor):
                reply_copy(k, k, j).start()

        @pl.when(jnp.logical_and(jnp.logical_not(first), k < 2))
        def _():
            for j in range(n_tensor):
                reply_copy(k, k + 2, j).start()

        @pl.when(jnp.logical_and(jnp.logical_not(first), k == 2))
        def _():
            final_copy().start()

        return carry

    lax.fori_loop(0, 4, step, 0)

    @pl.when(first)
    def _():
        far_phase(0)
        final_copy().wait_recv()
        out_ref[...] = final[...]
        for j in range(1, n_tensor):
            gather_copy(cot_hbm, 0, j, s).wait_send()
        for k in range(4):
            for j in range(n_tensor):
                reply_copy(k, k, j).wait_send()

    @pl.when(jnp.logical_not(first))
    def _():
        out_ref[...] = outs[3]
        final_copy().wait_send()
        for j in range(n_tensor):
            gather_copy(cot_hbm, 1, j, 1 - s).wait_send()
        for k in range(2):
            for j in range(n_tensor):
                reply_copy(k, k + 2, j).wait_send()

    last_phase(1)
    last_phase(0)
    for k in range(4):
        for j in range(1, n_tensor):
            reduce_copy(k, j).wait_send()
    for slot in range(2):
        core_copy(slot).wait_send()
        for j in range(1, NEAR):
            near_copy(slot, j).wait_send()
        for j in range(1, n_far):
            far_copy(slot, j).wait_send()


def on_device(
    n_tensor,
    n_dp,
    cotangent,
    saved_input,
    saved_normed,
    saved_query,
    saved_keyval,
    norm_gain,
    w_query,
    w_keyval,
    w_output,
):
    layers, _, micros, _, shard, width = saved_input.shape
    n_rows, q_width = saved_query.shape[4:]
    kv_width = w_keyval.shape[4]
    chunk = width // n_dp
    n_z = n_dp // 2
    n_far = n_z // NEAR
    items = layers * micros
    any_spec = pl.BlockSpec(memory_space=pl.ANY)
    vmem_spec = pl.BlockSpec(memory_space=pltpu.VMEM)
    dma = pltpu.SemaphoreType.DMA
    input_grad, keyval_grad = pl.pallas_call(
        functools.partial(kernel, n_tensor, n_dp),
        out_shape=(
            jax.ShapeDtypeStruct((shard, width), BF16),
            jax.ShapeDtypeStruct((layers, chunk, kv_width), F32),
        ),
        in_specs=[any_spec] * 9,
        out_specs=(vmem_spec, vmem_spec),
        scratch_shapes=[
            pltpu.VMEM((layers, micros, shard, width), BF16),
            pltpu.VMEM((layers, micros, n_rows, width), BF16),
            pltpu.VMEM((layers, micros, n_rows, q_width), BF16),
            pltpu.VMEM((layers, micros, n_rows, kv_width), BF16),
            pltpu.VMEM((layers, 1, width), F32),
            pltpu.VMEM((layers, width, q_width), BF16),
            pltpu.VMEM((layers, width, kv_width), BF16),
            pltpu.VMEM((layers, q_width, width), BF16),
            pltpu.VMEM((items, n_rows, width), BF16),
            pltpu.VMEM((items, n_rows, width), BF16),
            pltpu.VMEM((items, n_rows, width), BF16),
            pltpu.VMEM((items, shard, width), BF16),
            pltpu.VMEM((shard, width), BF16),
            pltpu.VMEM((layers, micros * n_rows, kv_width), BF16),
            pltpu.VMEM((layers, 2, width // 2, micros * n_rows), BF16),
            pltpu.VMEM((layers, width // 2, kv_width), BF16),
            pltpu.VMEM((layers, width // 2, kv_width), F32),
            pltpu.VMEM((layers, width // 2, kv_width), BF16),
            pltpu.VMEM((layers, NEAR, n_far * chunk, kv_width), BF16),
            pltpu.VMEM((layers, NEAR, n_far * chunk, kv_width), BF16),
            pltpu.VMEM((layers, n_far, chunk, kv_width), BF16),
            pltpu.VMEM((layers, n_far, chunk, kv_width), BF16),
            dma((8,)),
            dma((items, n_tensor)),
            dma((items, n_tensor)),
            dma((items, n_tensor)),
            dma((items, n_tensor)),
            dma((items, n_tensor)),
            dma(()),
            dma(()),
            dma((layers,)),
            dma((layers,)),
            dma((layers, NEAR)),
            dma((layers, NEAR)),
            dma((layers, n_far)),
            dma((layers, n_far)),
            pltpu.SemaphoreType.REGULAR,
            pltpu.SemaphoreType.REGULAR((3,)),
        ],
        compiler_params=pltpu.CompilerParams(
            collective_id=0, has_side_effects=True, vmem_limit_bytes=56 * 2**20
        ),
        name="backward",
    )(
        cotangent.reshape(shard, width),
        saved_input.reshape(layers, micros, shard, width),
        saved_normed.reshape(layers, micros, n_rows, width),
        saved_query.reshape(layers, micros, n_rows, q_width),
        saved_keyval.reshape(layers, micros, n_rows, kv_width),
        norm_gain,
        w_query.reshape(layers, width, q_width),
        w_keyval.reshape(layers, width, kv_width),
        w_output.reshape(layers, q_width, width),
    )
    return (
        input_grad[None, None],
        keyval_grad.reshape(layers, 1, chunk, 1, kv_width),
    )


def solution(mesh):
    in_specs = (
        P("section", "dp", "tensor", None),
        P(None, "section", None, "dp", "tensor", None),
        P(None, "section", None, "dp", None, None),
        P(None, "section", None, "dp", None, "tensor"),
        P(None, "section", None, "dp", None, "tensor", None),
        P(None, "section", None),
        P(None, "section", None, "tensor"),
        P(None, "section", None, "tensor", None),
        P(None, "section", "tensor", None),
    )
    out_specs = (P("section", "dp", "tensor", None), P(None, "section", "dp", "tensor", None))
    return jax.shard_map(
        functools.partial(on_device, mesh.shape["tensor"], mesh.shape["dp"]),
        mesh=mesh,
        in_specs=in_specs,
        out_specs=out_specs,
        check_vma=False,
    )
```

```python
import functools

import jax
import jax.numpy as jnp
from jax import lax
from jax.experimental import pallas as pl
from jax.experimental.pallas import tpu as pltpu
from jax.sharding import PartitionSpec as P

MESH = pl.DeviceIdType.MESH
BF16 = jnp.bfloat16
F32 = jnp.float32
NT = (((1,), (1,)), ((), ()))
TN = (((0,), (0,)), ((), ()))
NN = (((1,), (0,)), ((), ()))
NEAR = 4


def dot(a, b, dims):
    return lax.dot_general(a, b, dims, preferred_element_type=F32)


def attention_grads(query, keyval, d_attn, offset):
    rows, q_width = query.shape
    n_keys, lanes = keyval.shape
    head = lanes // 2
    scale = head**-0.5
    low = lax.broadcasted_iota(jnp.int32, (n_keys, lanes), 1) < head
    kv = keyval.astype(F32)
    vk = pltpu.roll(kv, head, 1)
    keys = jnp.concatenate(
        [jnp.where(low, kv * scale, 0.0), jnp.where(low, 0.0, vk * scale)], axis=0
    ).astype(BF16)
    values = jnp.concatenate([jnp.where(low, vk, 0.0), jnp.where(low, 0.0, kv)], axis=0).astype(BF16)

    def stacked(array):
        return jnp.concatenate(
            [array[:, p * lanes : (p + 1) * lanes] for p in range(q_width // lanes)], axis=0
        )

    query_st, d_attn_st = stacked(query), stacked(d_attn)
    scores = dot(keys, query_st, NT)
    d_share = dot(values, d_attn_st, NT)
    width = scores.shape[1]
    place = lax.broadcasted_iota(jnp.int32, (n_keys, width), 1) % rows + offset
    causal = lax.broadcasted_iota(jnp.int32, (n_keys, width), 0) <= place
    shares, d_scores = [], []
    for i in range(2):
        s = jnp.where(causal, scores[i * n_keys : (i + 1) * n_keys], -1e30)
        e = jnp.exp(s - jnp.max(s, axis=0, keepdims=True))
        p = e / jnp.sum(e, axis=0, keepdims=True)
        dp = d_share[i * n_keys : (i + 1) * n_keys]
        ds = p * (dp - jnp.sum(p * dp, axis=0, keepdims=True))
        shares.append(p.astype(BF16))
        d_scores.append(ds.astype(BF16))
    shares = jnp.concatenate(shares, axis=0)
    d_scores = jnp.concatenate(d_scores, axis=0)
    d_query_st = dot(d_scores, keys, TN).astype(BF16)
    d_query = jnp.concatenate(
        [d_query_st[p * rows : (p + 1) * rows] for p in range(q_width // lanes)], axis=1
    )
    dk = dot(d_scores, query_st, NN) * scale
    dv = dot(shares, d_attn_st, NN)
    d_keyval = jnp.where(low, dk[:n_keys], dv[n_keys:]) + pltpu.roll(
        jnp.where(low, dv[:n_keys], dk[n_keys:]), head, 1
    )
    return d_query, d_keyval


def folded(rows):
    half = rows.shape[1] // 2
    return jnp.concatenate([rows[:, :half], rows[:, half:]], axis=0)


def unfolded(rows):
    count = rows.shape[0] // 2
    return jnp.concatenate([rows[:count], rows[count:]], axis=1)


def kernel(
    n_tensor,
    n_dp,
    cot_hbm,
    xin_hbm,
    xn_hbm,
    q_hbm,
    kv_hbm,
    gain_hbm,
    wq_hbm,
    wkv_hbm,
    wo_hbm,
    out_ref,
    grad_ref,
    xin,
    xn,
    q,
    kv,
    gain,
    wq,
    wkv,
    wo,
    gathered,
    parts,
    landed,
    outs,
    final,
    cot,
    cot_folded,
    xf_out,
    xf,
    carried,
    dkv,
    turned,
    core_out,
    core_own,
    core_in,
    z1_out,
    z1_in,
    z2_out,
    z2_in,
    load_sem,
    ag_send,
    ag_recv,
    out_send,
    rs_send,
    rs_recv,
    fin_send,
    fin_recv,
    xf_send,
    xf_recv,
    core_send,
    core_recv,
    z1_send,
    z1_recv,
    z2_send,
    z2_recv,
    go_sem,
    token_sem,
):
    s = lax.axis_index("section")
    t = lax.axis_index("tensor")
    d = lax.axis_index("dp")
    z, core = d // 2, d % 2
    n_z = n_dp // 2
    n_far = n_z // NEAR
    zi, zg = z % NEAR, z // NEAR
    shard, half_width = outs.shape[2:]
    small = shard // 2
    n_rows = q.shape[2]
    half_rows = n_rows // 2
    home = t // (n_tensor // 2)
    chunk = grad_ref.shape[1]
    first = s == 1

    def tensor_peer(j):
        return lax.rem(t + j, n_tensor)

    def near_peer(j):
        return (zg * NEAR + lax.rem(zi + j, NEAR)) * 2 + core

    def far_peer(j):
        return (lax.rem(zg + j, n_far) * NEAR + zi) * 2 + core

    barrier = pltpu.get_barrier_semaphore()

    def hello(device):
        pl.semaphore_signal(barrier, inc=1, device_id=device, device_id_type=MESH)

    for j in range(1, n_tensor):
        hello({"tensor": tensor_peer(j)})
    for j in range(n_tensor):
        hello({"section": 1 - s, "tensor": tensor_peer(j)})
    hello({"dp": z * 2 + 1 - core})
    for j in range(1, NEAR):
        hello({"dp": near_peer(j)})
    for j in (1, n_far - 1):
        hello({"dp": far_peer(j)})

    loads = [
        pltpu.make_async_copy(src, dst, load_sem.at[i])
        for i, (src, dst) in enumerate(
            [
                (cot_hbm, cot),
                (xin_hbm, xin),
                (wo_hbm, wo),
                (q_hbm, q),
                (kv_hbm, kv),
                (wq_hbm, wq),
                (wkv_hbm, wkv),
                (gain_hbm, gain),
                (xn_hbm, xn),
            ]
        )
    ]
    for load in loads:
        load.start()

    loads[0].wait()
    for b in range(2):
        cot_folded[b] = folded(cot[...].astype(F32)[b * small : (b + 1) * small]).astype(BF16)
    loads[1].wait()
    for i in range(4):
        rows = xin[i // 2, i % 2].astype(F32)
        for b in range(2):
            xf_out[b, i] = folded(rows[b * small : (b + 1) * small]).astype(BF16)

    pl.semaphore_wait(barrier, 2 * n_tensor - 1 + 1 + NEAR - 1 + 2)

    def rows_of(index):
        return pl.ds(pl.multiple_of(index * shard, shard), shard)

    def block_of(b):
        return 2 * lax.rem(t, n_tensor // 2) + b

    def start_copy(item, b, j, section):
        return pltpu.make_async_remote_copy(
            src_ref=cot_folded.at[b],
            dst_ref=gathered.at[item, home, rows_of(block_of(b))],
            send_sem=ag_send.at[b, j],
            recv_sem=ag_recv.at[item, home, block_of(b)],
            device_id={"section": section, "tensor": tensor_peer(j)},
            device_id_type=MESH,
        )

    def own_shard_copy(b):
        return pltpu.make_async_copy(
            cot_folded.at[b],
            gathered.at[0, home, rows_of(block_of(b))],
            ag_recv.at[0, home, block_of(b)],
        )

    def reply_copy(k, h, item, j):
        return pltpu.make_async_remote_copy(
            src_ref=outs.at[k, h],
            dst_ref=gathered.at[item, h, rows_of(t)],
            send_sem=out_send.at[k, h, j],
            recv_sem=ag_recv.at[item, h, t],
            device_id={"section": 1 - s, "tensor": tensor_peer(j)},
            device_id_type=MESH,
        )

    def arrival(k, h, r):
        return pltpu.make_async_remote_copy(
            src_ref=outs.at[0, h],
            dst_ref=gathered.at[k, h, r * shard : (r + 1) * shard],
            send_sem=out_send.at[0, h, 0],
            recv_sem=ag_recv.at[k, h, r],
            device_id={"section": 1 - s},
            device_id_type=MESH,
        )

    def reduce_copy(k, h, j):
        return pltpu.make_async_remote_copy(
            src_ref=parts.at[k, h, rows_of(tensor_peer(j))],
            dst_ref=landed.at[k, h, rows_of(j)],
            send_sem=rs_send.at[k, h, j],
            recv_sem=rs_recv.at[k, h, j],
            device_id={"tensor": tensor_peer(j)},
            device_id_type=MESH,
        )

    def result_owner(h):
        return h * (n_tensor // 2) + t // 2

    def final_copy(k, h, section):
        return pltpu.make_async_remote_copy(
            src_ref=outs.at[k, h],
            dst_ref=final.at[t % 2],
            send_sem=fin_send.at[h],
            recv_sem=fin_recv.at[t % 2],
            device_id={"section": section, "tensor": result_owner(h)},
            device_id_type=MESH,
        )

    def final_last(h):
        return pltpu.make_async_remote_copy(
            src_ref=outs.at[3, h],
            dst_ref=final.at[t % 2],
            send_sem=fin_send.at[2 + h],
            recv_sem=fin_recv.at[t % 2],
            device_id={"tensor": result_owner(h)},
            device_id_type=MESH,
        )

    def final_own(k, h):
        return pltpu.make_async_copy(outs.at[k, h], final.at[t % 2], fin_recv.at[t % 2])

    def final_arrival(b):
        return pltpu.make_async_remote_copy(
            src_ref=outs.at[0, 0],
            dst_ref=final.at[b],
            send_sem=fin_send.at[0],
            recv_sem=fin_recv.at[b],
            device_id={"section": 1 - s},
            device_id_type=MESH,
        )

    def input_copy(b):
        return pltpu.make_async_remote_copy(
            src_ref=xf_out.at[b],
            dst_ref=xf.at[home],
            send_sem=xf_send.at[b],
            recv_sem=xf_recv.at[home],
            device_id={"tensor": block_of(b)},
            device_id_type=MESH,
        )

    def input_own(b):
        return pltpu.make_async_copy(xf_out.at[b], xf.at[home], xf_recv.at[home])

    def input_arrival(h):
        return pltpu.make_async_remote_copy(
            src_ref=xf_out.at[0],
            dst_ref=xf.at[h],
            send_sem=xf_send.at[0],
            recv_sem=xf_recv.at[h],
            device_id={"section": 1 - s},
            device_id_type=MESH,
        )

    def core_copy(slot):
        return pltpu.make_async_remote_copy(
            src_ref=core_out.at[slot],
            dst_ref=core_in.at[slot],
            send_sem=core_send.at[slot],
            recv_sem=core_recv.at[slot],
            device_id={"dp": z * 2 + 1 - core},
            device_id_type=MESH,
        )

    def near_copy(slot, j):
        return pltpu.make_async_remote_copy(
            src_ref=z1_out.at[slot, lax.rem(zi + j, NEAR)],
            dst_ref=z1_in.at[slot, j],
            send_sem=z1_send.at[slot, j],
            recv_sem=z1_recv.at[slot, j],
            device_id={"dp": near_peer(j)},
            device_id_type=MESH,
        )

    def far_copy(slot, j):
        return pltpu.make_async_remote_copy(
            src_ref=z2_out.at[slot, lax.rem(zg + j, n_far)],
            dst_ref=z2_in.at[slot, j],
            send_sem=z2_send.at[slot, j],
            recv_sem=z2_recv.at[slot, j],
            device_id={"dp": far_peer(j)},
            device_id_type=MESH,
        )

    def greet(round_index):
        for j in (1, n_far - 1):
            pl.semaphore_signal(
                token_sem.at[round_index],
                inc=1,
                device_id={"dp": far_peer(j)},
                device_id_type=MESH,
            )

    def greeted(round_index):
        pl.semaphore_wait(token_sem.at[round_index], 2)

    def turn(slot):
        def block(b, carry):
            columns = pl.ds(pl.multiple_of(b * 128, 128), 128)
            for place in range(2):
                flat = xn[slot, 1 - place, :, columns].T
                for i in range(128 // chunk):
                    owner = b * (128 // chunk) + i
                    oz, oc = owner // 2, owner % 2
                    where = (oz % NEAR) * n_far + oz // NEAR
                    turned[
                        slot,
                        oc,
                        pl.ds(pl.multiple_of(where * chunk, chunk), chunk),
                        place * n_rows : (place + 1) * n_rows,
                    ] = flat[i * chunk : (i + 1) * chunk]
            return carry

        lax.fori_loop(0, xn.shape[3] // 128, block, 0)

    def gradient(slot):
        rows = dkv[slot]

        def theirs(b, carry):
            span = pl.ds(pl.multiple_of(b * 256, 256), 256)
            core_out[slot, span] = dot(turned[slot, 1 - core, span], rows, NN).astype(BF16)
            return carry

        def ours(b, carry):
            span = pl.ds(pl.multiple_of(b * 256, 256), 256)
            core_own[slot, span] = dot(turned[slot, core, span], rows, NN)
            return carry

        count = core_out.shape[1] // 256
        lax.fori_loop(0, count, theirs, 0)
        core_copy(slot).start()
        lax.fori_loop(0, count, ours, 0)

    def near_phase(slot):
        core_copy(slot).wait_recv()
        block = n_far * chunk
        for i in range(NEAR):
            span = slice(i * block, (i + 1) * block)
            total = core_own[slot, span] + core_in[slot, span].astype(F32)
            core_own[slot, span] = total
            z1_out[slot, i] = total.astype(BF16)
        for j in range(1, NEAR):
            near_copy(slot, j).start()

    def far_phase(slot):
        block = n_far * chunk
        total = core_own[slot, pl.ds(pl.multiple_of(zi * block, block), block)]
        for j in range(1, NEAR):
            near_copy(slot, j).wait_recv()
            total = total + z1_in[slot, j].astype(F32)
        for g in range(n_far):
            piece = total[g * chunk : (g + 1) * chunk]
            z2_out[slot, g] = piece.astype(BF16)

            @pl.when(g == zg)
            def _():
                grad_ref[slot] = piece

        for j in range(1, n_far):
            far_copy(slot, j).start()

    def last_phase(slot):
        total = grad_ref[slot]
        for j in range(1, n_far):
            far_copy(slot, j).wait_recv()
            total = total + z2_in[slot, j].astype(F32)
        grad_ref[slot] = total

    @pl.when(first)
    def _():
        for b in range(2):
            own_shard_copy(b).start()
        for j in range(1, n_tensor):
            for b in range(2):
                start_copy(0, b, j, s).start()

    for b in range(2):

        @pl.when(block_of(b) != t)
        def _():
            input_copy(b).start()

        @pl.when(block_of(b) == t)
        def _():
            input_own(b).start()

    greet(0)
    for load in loads[2:]:
        load.wait()
    turn(1)

    @pl.when(jnp.logical_not(first))
    def _():
        pl.semaphore_wait(go_sem, 1)
        for j in range(n_tensor):
            for b in range(2):
                start_copy(1, b, j, 1 - s).start()

    def norm_half(k, h, slot, micro):
        x = xf[h, slot * 2 + micro].astype(F32)

        def over_rows(values):
            sums = jnp.sum(values, axis=-1, keepdims=True)
            mean = (sums[:small] + sums[small:]) / (2 * half_width)
            return jnp.concatenate([mean, mean], axis=0)

        r = lax.rsqrt(over_rows(x * x) + 1e-05)
        d_normed = parts[k, h, rows_of(t)].astype(F32)
        for j in range(1, n_tensor):
            reduce_copy(k, h, j).wait_recv()
            d_normed = d_normed + landed[k, h, j * shard : (j + 1) * shard].astype(F32)
        row = gain[slot]
        gains = jnp.concatenate(
            [
                jnp.broadcast_to(row[:, :half_width], (small, half_width)),
                jnp.broadcast_to(row[:, half_width:], (small, half_width)),
            ],
            axis=0,
        )
        scaled = d_normed * gains
        d_input = r * scaled - x * (r * r * r * over_rows(x * scaled))
        outs[k, h] = (gathered[k, h, rows_of(t)].astype(F32) + d_input).astype(BF16)

        @pl.when(first)
        def _():
            for j in range(n_tensor):
                reply_copy(k, h, k, j).start()

        @pl.when(jnp.logical_and(jnp.logical_not(first), k < 2))
        def _():
            for j in range(n_tensor):
                reply_copy(k, h, k + 2, j).start()

        @pl.when(jnp.logical_and(jnp.logical_not(first), k == 2))
        def _():
            final_copy(k, h, 1 - s).start()

        @pl.when(jnp.logical_and(jnp.logical_not(first), k == 3))
        def _():
            @pl.when(result_owner(h) != t)
            def _():
                final_last(h).start()

            @pl.when(result_owner(h) == t)
            def _():
                final_own(k, h).start()

    def step(k, carry):
        slot = 1 - k // 2
        place = k % 2
        micro = 1 - place
        tail = jnp.logical_and(k == 3, jnp.logical_not(first))
        for h in (1, 0):
            for r in range(n_tensor):
                arrival(k, h, r).wait_recv()
            low = dot(gathered[k, h], wo[slot, :, :half_width], NT)
            high = dot(gathered[k, h], wo[slot, :, half_width:], NT)
            d_attn = jnp.concatenate(
                [
                    low[r * shard : r * shard + small] + high[r * shard + small : (r + 1) * shard]
                    for r in range(n_tensor)
                ],
                axis=0,
            ).astype(BF16)
            base = h * half_rows
            d_query, d_keyval = attention_grads(
                q[slot, micro, base : base + half_rows],
                kv[slot, micro, : base + half_rows],
                d_attn,
                base,
            )
            if h:
                carried[...] = d_keyval[:half_rows]
                d_keyval = d_keyval[half_rows:].astype(BF16)
            else:
                d_keyval = (d_keyval + carried[...]).astype(BF16)
            dkv[slot, pl.ds(pl.multiple_of(place * n_rows + base, half_rows), half_rows)] = d_keyval

            if not h:

                @pl.when(tail)
                def _():
                    gradient(0)

            tile = half_width // 2
            for c in range(2):
                sides = []
                for side in range(2):
                    span = slice(side * half_width + c * tile, side * half_width + (c + 1) * tile)
                    sides.append(
                        dot(d_query, wq[slot, span], NT) + dot(d_keyval, wkv[slot, span], NT)
                    )
                blocks = []
                for r in range(n_tensor):
                    blocks += [side[r * small : (r + 1) * small] for side in sides]
                parts[k, h, :, c * tile : (c + 1) * tile] = jnp.concatenate(blocks, axis=0).astype(BF16)
            for j in range(1, n_tensor):
                reduce_copy(k, h, j).start()

        @pl.when(jnp.logical_and(first, k == 0))
        def _():
            pl.semaphore_signal(go_sem, inc=1, device_id={"section": 1 - s}, device_id_type=MESH)

        @pl.when(k == 0)
        def _():
            turn(0)
            for h in range(2):
                input_arrival(h).wait_recv()

        @pl.when(jnp.logical_and(place == 1, jnp.logical_not(tail)))
        def _():
            gradient(slot)

        @pl.when(place == 1)
        def _():
            near_phase(slot)

        @pl.when(k < 2)
        def _():
            greeted(k)
            greet(k + 1)

        @pl.when(k == 2)
        def _():
            greeted(2)
            far_phase(1)

        for h in (1, 0):
            norm_half(k, h, slot, micro)
        return carry

    lax.fori_loop(0, 4, step, 0)
    far_phase(0)
    for b in range(2):
        final_arrival(b).wait_recv()
    out_ref[...] = jnp.concatenate(
        [unfolded(final[b].astype(F32)) for b in range(2)], axis=0
    ).astype(BF16)

    @pl.when(first)
    def _():
        for j in range(1, n_tensor):
            for b in range(2):
                start_copy(0, b, j, s).wait_send()
        for k in range(4):
            for h in range(2):
                for j in range(n_tensor):
                    reply_copy(k, h, k, j).wait_send()

    @pl.when(jnp.logical_not(first))
    def _():
        for j in range(n_tensor):
            for b in range(2):
                start_copy(1, b, j, 1 - s).wait_send()
        for k in range(2):
            for h in range(2):
                for j in range(n_tensor):
                    reply_copy(k, h, k + 2, j).wait_send()
        for h in range(2):
            final_copy(2, h, 1 - s).wait_send()

            @pl.when(result_owner(h) != t)
            def _():
                final_last(h).wait_send()

    for b in range(2):

        @pl.when(block_of(b) != t)
        def _():
            input_copy(b).wait_send()

    last_phase(1)
    last_phase(0)
    for k in range(4):
        for h in range(2):
            for j in range(1, n_tensor):
                reduce_copy(k, h, j).wait_send()
    for slot in range(2):
        core_copy(slot).wait_send()
        for j in range(1, NEAR):
            near_copy(slot, j).wait_send()
        for j in range(1, n_far):
            far_copy(slot, j).wait_send()


def on_device(
    n_tensor,
    n_dp,
    cotangent,
    saved_input,
    saved_normed,
    saved_query,
    saved_keyval,
    norm_gain,
    w_query,
    w_keyval,
    w_output,
):
    layers, _, micros, _, shard, width = saved_input.shape
    n_rows, q_width = saved_query.shape[4:]
    kv_width = w_keyval.shape[4]
    chunk = width // n_dp
    n_z = n_dp // 2
    n_far = n_z // NEAR
    items = layers * micros
    any_spec = pl.BlockSpec(memory_space=pl.ANY)
    vmem_spec = pl.BlockSpec(memory_space=pltpu.VMEM)
    dma = pltpu.SemaphoreType.DMA
    input_grad, keyval_grad = pl.pallas_call(
        functools.partial(kernel, n_tensor, n_dp),
        out_shape=(
            jax.ShapeDtypeStruct((shard, width), BF16),
            jax.ShapeDtypeStruct((layers, chunk, kv_width), F32),
        ),
        in_specs=[any_spec] * 9,
        out_specs=(vmem_spec, vmem_spec),
        scratch_shapes=[
            pltpu.VMEM((layers, micros, shard, width), BF16),
            pltpu.VMEM((layers, micros, n_rows, width), BF16),
            pltpu.VMEM((layers, micros, n_rows, q_width), BF16),
            pltpu.VMEM((layers, micros, n_rows, kv_width), BF16),
            pltpu.VMEM((layers, 1, width), F32),
            pltpu.VMEM((layers, width, q_width), BF16),
            pltpu.VMEM((layers, width, kv_width), BF16),
            pltpu.VMEM((layers, q_width, width), BF16),
            pltpu.VMEM((items, 2, n_rows, width // 2), BF16),
            pltpu.VMEM((items, 2, n_rows, width // 2), BF16),
            pltpu.VMEM((items, 2, n_rows, width // 2), BF16),
            pltpu.VMEM((items, 2, shard, width // 2), BF16),
            pltpu.VMEM((2, shard, width // 2), BF16),
            pltpu.VMEM((shard, width), BF16),
            pltpu.VMEM((2, shard, width // 2), BF16),
            pltpu.VMEM((2, items, shard, width // 2), BF16),
            pltpu.VMEM((2, items, shard, width // 2), BF16),
            pltpu.VMEM((n_rows // 2, kv_width), F32),
            pltpu.VMEM((layers, micros * n_rows, kv_width), BF16),
            pltpu.VMEM((layers, 2, width // 2, micros * n_rows), BF16),
            pltpu.VMEM((layers, width // 2, kv_width), BF16),
            pltpu.VMEM((layers, width // 2, kv_width), F32),
            pltpu.VMEM((layers, width // 2, kv_width), BF16),
            pltpu.VMEM((layers, NEAR, n_far * chunk, kv_width), BF16),
            pltpu.VMEM((layers, NEAR, n_far * chunk, kv_width), BF16),
            pltpu.VMEM((layers, n_far, chunk, kv_width), BF16),
            pltpu.VMEM((layers, n_far, chunk, kv_width), BF16),
            dma((9,)),
            dma((2, n_tensor)),
            dma((items, 2, n_tensor)),
            dma((items, 2, n_tensor)),
            dma((items, 2, n_tensor)),
            dma((items, 2, n_tensor)),
            dma((4,)),
            dma((2,)),
            dma((2,)),
            dma((2,)),
            dma((layers,)),
            dma((layers,)),
            dma((layers, NEAR)),
            dma((layers, NEAR)),
            dma((layers, n_far)),
            dma((layers, n_far)),
            pltpu.SemaphoreType.REGULAR,
            pltpu.SemaphoreType.REGULAR((3,)),
        ],
        compiler_params=pltpu.CompilerParams(
            collective_id=0, has_side_effects=True, vmem_limit_bytes=56 * 2**20
        ),
        name="backward",
    )(
        cotangent.reshape(shard, width),
        saved_input.reshape(layers, micros, shard, width),
        saved_normed.reshape(layers, micros, n_rows, width),
        saved_query.reshape(layers, micros, n_rows, q_width),
        saved_keyval.reshape(layers, micros, n_rows, kv_width),
        norm_gain,
        w_query.reshape(layers, width, q_width),
        w_keyval.reshape(layers, width, kv_width),
        w_output.reshape(layers, q_width, width),
    )
    return (
        input_grad[None, None],
        keyval_grad.reshape(layers, 1, chunk, 1, kv_width),
    )


def solution(mesh):
    in_specs = (
        P("section", "dp", "tensor", None),
        P(None, "section", None, "dp", "tensor", None),
        P(None, "section", None, "dp", None, None),
        P(None, "section", None, "dp", None, "tensor"),
        P(None, "section", None, "dp", None, "tensor", None),
        P(None, "section", None),
        P(None, "section", None, "tensor"),
        P(None, "section", None, "tensor", None),
        P(None, "section", "tensor", None),
    )
    out_specs = (P("section", "dp", "tensor", None), P(None, "section", "dp", "tensor", None))
    return jax.shard_map(
        functools.partial(on_device, mesh.shape["tensor"], mesh.shape["dp"]),
        mesh=mesh,
        in_specs=in_specs,
        out_specs=out_specs,
        check_vma=False,
    )
```

```python
import functools

import jax
import jax.numpy as jnp
from jax import lax
from jax.experimental import pallas as pl
from jax.experimental.pallas import tpu as pltpu
from jax.sharding import PartitionSpec as P

MESH = pl.DeviceIdType.MESH
BF16 = jnp.bfloat16
F32 = jnp.float32
NT = (((1,), (1,)), ((), ()))
TN = (((0,), (0,)), ((), ()))
NN = (((1,), (0,)), ((), ()))
NEAR = 4


def dot(a, b, dims):
    return lax.dot_general(a, b, dims, preferred_element_type=F32)


def attention_grads(query, keyval, d_attn, offset):
    rows, q_width = query.shape
    n_keys, lanes = keyval.shape
    head = lanes // 2
    scale = head**-0.5
    low = lax.broadcasted_iota(jnp.int32, (n_keys, lanes), 1) < head
    kv = keyval.astype(F32)
    vk = pltpu.roll(kv, head, 1)
    keys = jnp.concatenate(
        [jnp.where(low, kv * scale, 0.0), jnp.where(low, 0.0, vk * scale)], axis=0
    ).astype(BF16)
    values = jnp.concatenate([jnp.where(low, vk, 0.0), jnp.where(low, 0.0, kv)], axis=0).astype(BF16)

    def stacked(array):
        return jnp.concatenate(
            [array[:, p * lanes : (p + 1) * lanes] for p in range(q_width // lanes)], axis=0
        )

    query_st, d_attn_st = stacked(query), stacked(d_attn)
    scores = dot(keys, query_st, NT)
    d_share = dot(values, d_attn_st, NT)
    width = scores.shape[1]
    place = lax.broadcasted_iota(jnp.int32, (n_keys, width), 1) % rows + offset
    causal = lax.broadcasted_iota(jnp.int32, (n_keys, width), 0) <= place
    shares, d_scores = [], []
    for i in range(2):
        s = jnp.where(causal, scores[i * n_keys : (i + 1) * n_keys], -1e30)
        e = jnp.exp(s - jnp.max(s, axis=0, keepdims=True))
        p = e / jnp.sum(e, axis=0, keepdims=True)
        dp = d_share[i * n_keys : (i + 1) * n_keys]
        ds = p * (dp - jnp.sum(p * dp, axis=0, keepdims=True))
        shares.append(p.astype(BF16))
        d_scores.append(ds.astype(BF16))
    shares = jnp.concatenate(shares, axis=0)
    d_scores = jnp.concatenate(d_scores, axis=0)
    d_query_st = dot(d_scores, keys, TN).astype(BF16)
    d_query = jnp.concatenate(
        [d_query_st[p * rows : (p + 1) * rows] for p in range(q_width // lanes)], axis=1
    )
    dk = dot(d_scores, query_st, NN) * scale
    dv = dot(shares, d_attn_st, NN)
    d_keyval = jnp.where(low, dk[:n_keys], dv[n_keys:]) + pltpu.roll(
        jnp.where(low, dv[:n_keys], dk[n_keys:]), head, 1
    )
    return d_query, d_keyval


def folded(rows):
    half = rows.shape[1] // 2
    return jnp.concatenate([rows[:, :half], rows[:, half:]], axis=0)


def unfolded(rows):
    count = rows.shape[0] // 2
    return jnp.concatenate([rows[:count], rows[count:]], axis=1)


def kernel(
    n_tensor,
    n_dp,
    cot_hbm,
    xin_hbm,
    xn_hbm,
    q_hbm,
    kv_hbm,
    gain_hbm,
    wq_hbm,
    wkv_hbm,
    wo_hbm,
    out_ref,
    grad_ref,
    xin,
    xn,
    q,
    kv,
    gain,
    wq,
    wkv,
    wo,
    gathered,
    parts,
    landed,
    outs,
    final,
    cot,
    cot_folded,
    xf_out,
    xf,
    carried,
    kept,
    dkv,
    turned,
    core_out,
    core_own,
    core_in,
    z1_out,
    z1_in,
    z2_out,
    z2_in,
    load_sem,
    ag_send,
    ag_recv,
    out_send,
    rs_send,
    rs_recv,
    fin_send,
    fin_recv,
    xf_send,
    xf_recv,
    core_send,
    core_recv,
    z1_send,
    z1_recv,
    z2_send,
    z2_recv,
    go_sem,
    token_sem,
):
    s = lax.axis_index("section")
    t = lax.axis_index("tensor")
    d = lax.axis_index("dp")
    z, core = d // 2, d % 2
    n_z = n_dp // 2
    n_far = n_z // NEAR
    zi, zg = z % NEAR, z // NEAR
    shard, half_width = outs.shape[2:]
    small = shard // 2
    n_rows = q.shape[2]
    half_rows = n_rows // 2
    home = t // (n_tensor // 2)
    chunk = grad_ref.shape[1]
    first = s == 1

    n_x = n_tensor // 2
    ty, tx = t // n_x, lax.rem(t, n_x)

    def tensor_peer(j):
        return lax.rem(ty + j // n_x, 2) * n_x + lax.rem(tx + j % n_x, n_x)

    def distance(j):
        return 2 * (j // n_x) + min(j % n_x, n_x - j % n_x)

    others = sorted(range(1, n_tensor), key=lambda j: -distance(j))
    everyone = sorted(range(n_tensor), key=lambda j: -min(j % n_x, n_x - j % n_x))

    def near_peer(j):
        return (zg * NEAR + lax.rem(zi + j, NEAR)) * 2 + core

    def far_peer(j):
        return (lax.rem(zg + j, n_far) * NEAR + zi) * 2 + core

    barrier = pltpu.get_barrier_semaphore()

    def hello(device):
        pl.semaphore_signal(barrier, inc=1, device_id=device, device_id_type=MESH)

    for j in range(1, n_tensor):
        hello({"tensor": tensor_peer(j)})
    for j in range(n_tensor):
        hello({"section": 1 - s, "tensor": tensor_peer(j)})
    hello({"dp": z * 2 + 1 - core})
    for j in range(1, NEAR):
        hello({"dp": near_peer(j)})
    for j in (1, n_far - 1):
        hello({"dp": far_peer(j)})

    loads = [
        pltpu.make_async_copy(src, dst, load_sem.at[i])
        for i, (src, dst) in enumerate(
            [
                (cot_hbm, cot),
                (xin_hbm, xin),
                (wo_hbm, wo),
                (q_hbm, q),
                (kv_hbm, kv),
                (wq_hbm, wq),
                (wkv_hbm, wkv),
                (gain_hbm, gain),
                (xn_hbm, xn),
            ]
        )
    ]
    for load in loads:
        load.start()

    loads[0].wait()
    for b in range(2):
        cot_folded[b] = folded(cot[...].astype(F32)[b * small : (b + 1) * small]).astype(BF16)
    loads[1].wait()
    for i in range(4):
        rows = xin[i // 2, i % 2].astype(F32)
        for b in range(2):
            xf_out[b, i] = folded(rows[b * small : (b + 1) * small]).astype(BF16)

    pl.semaphore_wait(barrier, 2 * n_tensor - 1 + 1 + NEAR - 1 + 2)

    def rows_of(index):
        return pl.ds(pl.multiple_of(index * shard, shard), shard)

    def block_of(b):
        return 2 * lax.rem(t, n_tensor // 2) + b

    def start_copy(item, b, j, section):
        return pltpu.make_async_remote_copy(
            src_ref=cot_folded.at[b],
            dst_ref=gathered.at[item, home, rows_of(block_of(b))],
            send_sem=ag_send.at[b, j],
            recv_sem=ag_recv.at[item, home, block_of(b)],
            device_id={"section": section, "tensor": tensor_peer(j)},
            device_id_type=MESH,
        )

    def own_shard_copy(b):
        return pltpu.make_async_copy(
            cot_folded.at[b],
            gathered.at[0, home, rows_of(block_of(b))],
            ag_recv.at[0, home, block_of(b)],
        )

    def reply_copy(k, h, item, j):
        return pltpu.make_async_remote_copy(
            src_ref=outs.at[k, h],
            dst_ref=gathered.at[item, h, rows_of(t)],
            send_sem=out_send.at[k, h, j],
            recv_sem=ag_recv.at[item, h, t],
            device_id={"section": 1 - s, "tensor": tensor_peer(j)},
            device_id_type=MESH,
        )

    def arrival(k, h, r):
        return pltpu.make_async_remote_copy(
            src_ref=outs.at[0, h],
            dst_ref=gathered.at[k, h, r * shard : (r + 1) * shard],
            send_sem=out_send.at[0, h, 0],
            recv_sem=ag_recv.at[k, h, r],
            device_id={"section": 1 - s},
            device_id_type=MESH,
        )

    def reduce_copy(k, h, j):
        return pltpu.make_async_remote_copy(
            src_ref=parts.at[k, h, rows_of(tensor_peer(j))],
            dst_ref=landed.at[k, h, rows_of(j)],
            send_sem=rs_send.at[k, h, j],
            recv_sem=rs_recv.at[k, h, j],
            device_id={"tensor": tensor_peer(j)},
            device_id_type=MESH,
        )

    def result_owner(h):
        return h * (n_tensor // 2) + t // 2

    def final_copy(k, h, section):
        return pltpu.make_async_remote_copy(
            src_ref=outs.at[k, h],
            dst_ref=final.at[t % 2],
            send_sem=fin_send.at[h],
            recv_sem=fin_recv.at[t % 2],
            device_id={"section": section, "tensor": result_owner(h)},
            device_id_type=MESH,
        )

    def final_last(h):
        return pltpu.make_async_remote_copy(
            src_ref=outs.at[3, h],
            dst_ref=final.at[t % 2],
            send_sem=fin_send.at[2 + h],
            recv_sem=fin_recv.at[t % 2],
            device_id={"tensor": result_owner(h)},
            device_id_type=MESH,
        )

    def final_own(k, h):
        return pltpu.make_async_copy(outs.at[k, h], final.at[t % 2], fin_recv.at[t % 2])

    def final_arrival(b):
        return pltpu.make_async_remote_copy(
            src_ref=outs.at[0, 0],
            dst_ref=final.at[b],
            send_sem=fin_send.at[0],
            recv_sem=fin_recv.at[b],
            device_id={"section": 1 - s},
            device_id_type=MESH,
        )

    def input_copy(b):
        return pltpu.make_async_remote_copy(
            src_ref=xf_out.at[b],
            dst_ref=xf.at[home],
            send_sem=xf_send.at[b],
            recv_sem=xf_recv.at[home],
            device_id={"tensor": block_of(b)},
            device_id_type=MESH,
        )

    def input_own(b):
        return pltpu.make_async_copy(xf_out.at[b], xf.at[home], xf_recv.at[home])

    def input_arrival(h):
        return pltpu.make_async_remote_copy(
            src_ref=xf_out.at[0],
            dst_ref=xf.at[h],
            send_sem=xf_send.at[0],
            recv_sem=xf_recv.at[h],
            device_id={"section": 1 - s},
            device_id_type=MESH,
        )

    def core_copy(slot):
        return pltpu.make_async_remote_copy(
            src_ref=core_out.at[slot],
            dst_ref=core_in.at[slot],
            send_sem=core_send.at[slot],
            recv_sem=core_recv.at[slot],
            device_id={"dp": z * 2 + 1 - core},
            device_id_type=MESH,
        )

    def near_copy(slot, part, j):
        span = pl.ds(part * (n_far // 2), n_far // 2)
        return pltpu.make_async_remote_copy(
            src_ref=z1_out.at[slot, lax.rem(zi + j, NEAR), span],
            dst_ref=z1_in.at[slot, j, span],
            send_sem=z1_send.at[slot, part, j],
            recv_sem=z1_recv.at[slot, part, j],
            device_id={"dp": near_peer(j)},
            device_id_type=MESH,
        )

    def far_copy(slot, j):
        return pltpu.make_async_remote_copy(
            src_ref=z2_out.at[slot, j],
            dst_ref=z2_in.at[slot, j],
            send_sem=z2_send.at[slot, j],
            recv_sem=z2_recv.at[slot, j],
            device_id={"dp": far_peer(j)},
            device_id_type=MESH,
        )

    def greet(round_index):
        for j in (1, n_far - 1):
            pl.semaphore_signal(
                token_sem.at[round_index],
                inc=1,
                device_id={"dp": far_peer(j)},
                device_id_type=MESH,
            )

    def greeted(round_index):
        pl.semaphore_wait(token_sem.at[round_index], 2)

    def turn(slot):
        def block(b, carry):
            columns = pl.ds(pl.multiple_of(b * 128, 128), 128)
            for place in range(2):
                flat = xn[slot, 1 - place, :, columns].T
                for i in range(128 // chunk):
                    owner = b * (128 // chunk) + i
                    oz, oc = owner // 2, owner % 2
                    where = (oz % NEAR) * n_far + oz // NEAR
                    turned[
                        slot,
                        oc,
                        pl.ds(pl.multiple_of(where * chunk, chunk), chunk),
                        place * n_rows : (place + 1) * n_rows,
                    ] = flat[i * chunk : (i + 1) * chunk]
            return carry

        lax.fori_loop(0, xn.shape[3] // 128, block, 0)

    def gradient(slot):
        rows = dkv[slot]

        def theirs(b, carry):
            span = pl.ds(pl.multiple_of(b * 256, 256), 256)
            core_out[slot, span] = dot(turned[slot, 1 - core, span], rows, NN).astype(BF16)
            return carry

        def ours(b, carry):
            span = pl.ds(pl.multiple_of(b * 256, 256), 256)
            core_own[slot, span] = dot(turned[slot, core, span], rows, NN)
            return carry

        count = core_out.shape[1] // 256
        lax.fori_loop(0, count, theirs, 0)
        core_copy(slot).start()
        lax.fori_loop(0, count, ours, 0)

    far_order = [(i + n_far // 4) % n_far for i in range(n_far)]

    def sum_rows(i, j):
        where = (i * n_far + lax.rem(zg + j, n_far)) * chunk
        return pl.ds(pl.multiple_of(where, chunk), chunk)

    def near_phase(slot):
        core_copy(slot).wait_recv()
        for part in range(2):
            for i in range(NEAR):
                for place in range(part * (n_far // 2), (part + 1) * (n_far // 2)):
                    span = sum_rows(i, far_order[place])
                    total = core_own[slot, span] + core_in[slot, span].astype(F32)
                    core_own[slot, span] = total
                    z1_out[slot, i, place] = total.astype(BF16)
            for j in range(1, NEAR):
                near_copy(slot, part, j).start()

    def far_phase(slot, part):
        for j in range(1, NEAR):
            near_copy(slot, part, j).wait_recv()
        places = range(part * (n_far // 2), (part + 1) * (n_far // 2))
        for place in sorted(places, key=lambda p: abs(far_order[p] - n_far // 2)):
            j = far_order[place]
            total = core_own[slot, sum_rows(zi, j)]
            for i in range(1, NEAR):
                total = total + z1_in[slot, i, place].astype(F32)
            if j:
                z2_out[slot, j] = total.astype(BF16)
                far_copy(slot, j).start()
            else:
                grad_ref[slot] = total

    def last_phase(slot):
        total = grad_ref[slot]
        for j in range(1, n_far):
            far_copy(slot, j).wait_recv()
            total = total + z2_in[slot, j].astype(F32)
        grad_ref[slot] = total

    @pl.when(first)
    def _():
        for b in range(2):
            own_shard_copy(b).start()
        for j in others:
            for b in range(2):
                start_copy(0, b, j, s).start()

    for b in range(2):

        @pl.when(block_of(b) != t)
        def _():
            input_copy(b).start()

        @pl.when(block_of(b) == t)
        def _():
            input_own(b).start()

    greet(0)
    for load in loads[2:]:
        load.wait()
    turn(1)

    @pl.when(jnp.logical_not(first))
    def _():
        pl.semaphore_wait(go_sem, 1)
        for j in range(n_tensor):
            for b in range(2):
                start_copy(1, b, j, 1 - s).start()

    def norm_half(k, h, slot, micro):
        x = xf[h, slot * 2 + micro].astype(F32)

        def over_rows(values):
            sums = jnp.sum(values, axis=-1, keepdims=True)
            mean = (sums[:small] + sums[small:]) / (2 * half_width)
            return jnp.concatenate([mean, mean], axis=0)

        r = lax.rsqrt(over_rows(x * x) + 1e-05)
        d_normed = parts[k, h, rows_of(t)].astype(F32)
        for j in range(1, n_tensor):
            reduce_copy(k, h, j).wait_recv()
            d_normed = d_normed + landed[k, h, j * shard : (j + 1) * shard].astype(F32)
        row = gain[slot]
        gains = jnp.concatenate(
            [
                jnp.broadcast_to(row[:, :half_width], (small, half_width)),
                jnp.broadcast_to(row[:, half_width:], (small, half_width)),
            ],
            axis=0,
        )
        scaled = d_normed * gains
        d_input = r * scaled - x * (r * r * r * over_rows(x * scaled))
        outs[k, h] = (gathered[k, h, rows_of(t)].astype(F32) + d_input).astype(BF16)

        @pl.when(first)
        def _():
            for j in everyone:
                reply_copy(k, h, k, j).start()

        @pl.when(jnp.logical_and(jnp.logical_not(first), k < 2))
        def _():
            for j in everyone:
                reply_copy(k, h, k + 2, j).start()

        @pl.when(jnp.logical_and(jnp.logical_not(first), k == 2))
        def _():
            final_copy(k, h, 1 - s).start()

        @pl.when(jnp.logical_and(jnp.logical_not(first), k == 3))
        def _():
            @pl.when(result_owner(h) != t)
            def _():
                final_last(h).start()

            @pl.when(result_owner(h) == t)
            def _():
                final_own(k, h).start()

    def kv_rows(h, place):
        start = place * n_rows + h * half_rows
        return pl.ds(pl.multiple_of(start, half_rows), half_rows)

    def project(k, h, slot, place):
        d_query, d_keyval = kept[h], dkv[slot, kv_rows(h, place)]
        tile = half_width // 2
        for c in range(2):
            sides = []
            for side in range(2):
                span = slice(side * half_width + c * tile, side * half_width + (c + 1) * tile)
                sides.append(dot(d_query, wq[slot, span], NT) + dot(d_keyval, wkv[slot, span], NT))
            blocks = []
            for r in range(n_tensor):
                blocks += [side[r * small : (r + 1) * small] for side in sides]
            parts[k, h, :, c * tile : (c + 1) * tile] = jnp.concatenate(blocks, axis=0).astype(BF16)

    def scatter(k, h):
        for j in others:
            reduce_copy(k, h, j).start()

    def step(k, carry):
        slot = 1 - k // 2
        place = k % 2
        micro = 1 - place
        tail = jnp.logical_and(k == 3, jnp.logical_not(first))
        for h in (1, 0):
            for r in range(n_tensor):
                arrival(k, h, r).wait_recv()
            low = dot(gathered[k, h], wo[slot, :, :half_width], NT)
            high = dot(gathered[k, h], wo[slot, :, half_width:], NT)
            d_attn = jnp.concatenate(
                [
                    low[r * shard : r * shard + small] + high[r * shard + small : (r + 1) * shard]
                    for r in range(n_tensor)
                ],
                axis=0,
            ).astype(BF16)
            base = h * half_rows
            d_query, d_keyval = attention_grads(
                q[slot, micro, base : base + half_rows],
                kv[slot, micro, : base + half_rows],
                d_attn,
                base,
            )
            if h:
                carried[...] = d_keyval[:half_rows]
                d_keyval = d_keyval[half_rows:].astype(BF16)
            else:
                d_keyval = (d_keyval + carried[...]).astype(BF16)
            dkv[slot, kv_rows(h, place)] = d_keyval
            kept[h] = d_query
            if h:

                @pl.when(jnp.logical_not(tail))
                def _():
                    project(k, 1, slot, place)
                    scatter(k, 1)

            else:

                @pl.when(tail)
                def _():
                    gradient(0)
                    project(k, 1, slot, place)
                    scatter(k, 1)

                project(k, 0, slot, place)

                @pl.when(tail)
                def _():
                    near_phase(0)

                scatter(k, 0)

        @pl.when(jnp.logical_and(first, k == 0))
        def _():
            pl.semaphore_signal(go_sem, inc=1, device_id={"section": 1 - s}, device_id_type=MESH)

        @pl.when(k == 0)
        def _():
            turn(0)
            for h in range(2):
                input_arrival(h).wait_recv()

        @pl.when(jnp.logical_and(place == 1, jnp.logical_not(tail)))
        def _():
            gradient(slot)

        @pl.when(k < 2)
        def _():
            greeted(k)
            greet(k + 1)

        @pl.when(tail)
        def _():
            far_phase(0, 0)

        norm_half(k, 1, slot, micro)

        @pl.when(tail)
        def _():
            far_phase(0, 1)

        norm_half(k, 0, slot, micro)

        @pl.when(jnp.logical_and(place == 1, jnp.logical_not(tail)))
        def _():
            near_phase(slot)

        @pl.when(k == 2)
        def _():
            greeted(2)
            far_phase(1, 0)
            far_phase(1, 1)

        return carry

    lax.fori_loop(0, 4, step, 0)

    @pl.when(first)
    def _():
        far_phase(0, 0)
        far_phase(0, 1)

    for b in range(2):
        final_arrival(b).wait_recv()
    out_ref[...] = jnp.concatenate(
        [unfolded(final[b].astype(F32)) for b in range(2)], axis=0
    ).astype(BF16)

    @pl.when(first)
    def _():
        for j in range(1, n_tensor):
            for b in range(2):
                start_copy(0, b, j, s).wait_send()
        for k in range(4):
            for h in range(2):
                for j in range(n_tensor):
                    reply_copy(k, h, k, j).wait_send()

    @pl.when(jnp.logical_not(first))
    def _():
        for j in range(n_tensor):
            for b in range(2):
                start_copy(1, b, j, 1 - s).wait_send()
        for k in range(2):
            for h in range(2):
                for j in range(n_tensor):
                    reply_copy(k, h, k + 2, j).wait_send()
        for h in range(2):
            final_copy(2, h, 1 - s).wait_send()

            @pl.when(result_owner(h) != t)
            def _():
                final_last(h).wait_send()

    for b in range(2):

        @pl.when(block_of(b) != t)
        def _():
            input_copy(b).wait_send()

    last_phase(1)
    last_phase(0)
    for k in range(4):
        for h in range(2):
            for j in range(1, n_tensor):
                reduce_copy(k, h, j).wait_send()
    for slot in range(2):
        core_copy(slot).wait_send()
        for part in range(2):
            for j in range(1, NEAR):
                near_copy(slot, part, j).wait_send()
        for j in range(1, n_far):
            far_copy(slot, j).wait_send()


def handed_on(rows_ref, grad_ref, rows_out, grad_out, sems):
    copies = [
        pltpu.make_async_copy(rows_ref, rows_out, sems.at[0]),
        pltpu.make_async_copy(grad_ref, grad_out, sems.at[1]),
    ]
    for copy in copies:
        copy.start()
    for copy in copies:
        copy.wait()


def on_device(
    n_tensor,
    n_dp,
    cotangent,
    saved_input,
    saved_normed,
    saved_query,
    saved_keyval,
    norm_gain,
    w_query,
    w_keyval,
    w_output,
):
    layers, _, micros, _, shard, width = saved_input.shape
    n_rows, q_width = saved_query.shape[4:]
    kv_width = w_keyval.shape[4]
    chunk = width // n_dp
    n_z = n_dp // 2
    n_far = n_z // NEAR
    items = layers * micros
    any_spec = pl.BlockSpec(memory_space=pl.ANY)
    vmem_spec = pl.BlockSpec(memory_space=pltpu.VMEM)
    dma = pltpu.SemaphoreType.DMA
    input_grad, keyval_grad = pl.pallas_call(
        functools.partial(kernel, n_tensor, n_dp),
        out_shape=(
            jax.ShapeDtypeStruct((shard, width), BF16),
            jax.ShapeDtypeStruct((layers, chunk, kv_width), F32),
        ),
        in_specs=[any_spec] * 9,
        out_specs=(vmem_spec, vmem_spec),
        scratch_shapes=[
            pltpu.VMEM((layers, micros, shard, width), BF16),
            pltpu.VMEM((layers, micros, n_rows, width), BF16),
            pltpu.VMEM((layers, micros, n_rows, q_width), BF16),
            pltpu.VMEM((layers, micros, n_rows, kv_width), BF16),
            pltpu.VMEM((layers, 1, width), F32),
            pltpu.VMEM((layers, width, q_width), BF16),
            pltpu.VMEM((layers, width, kv_width), BF16),
            pltpu.VMEM((layers, q_width, width), BF16),
            pltpu.VMEM((items, 2, n_rows, width // 2), BF16),
            pltpu.VMEM((items, 2, n_rows, width // 2), BF16),
            pltpu.VMEM((items, 2, n_rows, width // 2), BF16),
            pltpu.VMEM((items, 2, shard, width // 2), BF16),
            pltpu.VMEM((2, shard, width // 2), BF16),
            pltpu.VMEM((shard, width), BF16),
            pltpu.VMEM((2, shard, width // 2), BF16),
            pltpu.VMEM((2, items, shard, width // 2), BF16),
            pltpu.VMEM((2, items, shard, width // 2), BF16),
            pltpu.VMEM((n_rows // 2, kv_width), F32),
            pltpu.VMEM((2, n_rows // 2, q_width), BF16),
            pltpu.VMEM((layers, micros * n_rows, kv_width), BF16),
            pltpu.VMEM((layers, 2, width // 2, micros * n_rows), BF16),
            pltpu.VMEM((layers, width // 2, kv_width), BF16),
            pltpu.VMEM((layers, width // 2, kv_width), F32),
            pltpu.VMEM((layers, width // 2, kv_width), BF16),
            pltpu.VMEM((layers, NEAR, n_far, chunk, kv_width), BF16),
            pltpu.VMEM((layers, NEAR, n_far, chunk, kv_width), BF16),
            pltpu.VMEM((layers, n_far, chunk, kv_width), BF16),
            pltpu.VMEM((layers, n_far, chunk, kv_width), BF16),
            dma((9,)),
            dma((2, n_tensor)),
            dma((items, 2, n_tensor)),
            dma((items, 2, n_tensor)),
            dma((items, 2, n_tensor)),
            dma((items, 2, n_tensor)),
            dma((4,)),
            dma((2,)),
            dma((2,)),
            dma((2,)),
            dma((layers,)),
            dma((layers,)),
            dma((layers, 2, NEAR)),
            dma((layers, 2, NEAR)),
            dma((layers, n_far)),
            dma((layers, n_far)),
            pltpu.SemaphoreType.REGULAR,
            pltpu.SemaphoreType.REGULAR((3,)),
        ],
        compiler_params=pltpu.CompilerParams(
            collective_id=0, has_side_effects=True, vmem_limit_bytes=56 * 2**20
        ),
        name="backward",
    )(
        cotangent.reshape(shard, width),
        saved_input.reshape(layers, micros, shard, width),
        saved_normed.reshape(layers, micros, n_rows, width),
        saved_query.reshape(layers, micros, n_rows, q_width),
        saved_keyval.reshape(layers, micros, n_rows, kv_width),
        norm_gain,
        w_query.reshape(layers, width, q_width),
        w_keyval.reshape(layers, width, kv_width),
        w_output.reshape(layers, q_width, width),
    )
    input_grad, keyval_grad = pl.pallas_call(
        handed_on,
        out_shape=(
            jax.ShapeDtypeStruct(input_grad.shape, BF16),
            jax.ShapeDtypeStruct(keyval_grad.shape, F32),
        ),
        in_specs=[any_spec] * 2,
        out_specs=(any_spec, any_spec),
        scratch_shapes=[dma((2,))],
        name="results",
    )(input_grad, keyval_grad)
    return (
        input_grad[None, None],
        keyval_grad.reshape(layers, 1, chunk, 1, kv_width),
    )


def solution(mesh):
    in_specs = (
        P("section", "dp", "tensor", None),
        P(None, "section", None, "dp", "tensor", None),
        P(None, "section", None, "dp", None, None),
        P(None, "section", None, "dp", None, "tensor"),
        P(None, "section", None, "dp", None, "tensor", None),
        P(None, "section", None),
        P(None, "section", None, "tensor"),
        P(None, "section", None, "tensor", None),
        P(None, "section", "tensor", None),
    )
    out_specs = (P("section", "dp", "tensor", None), P(None, "section", "dp", "tensor", None))
    return jax.shard_map(
        functools.partial(on_device, mesh.shape["tensor"], mesh.shape["dp"]),
        mesh=mesh,
        in_specs=in_specs,
        out_specs=out_specs,
        check_vma=False,
    )
```

```python
import functools

import jax
import jax.numpy as jnp
from jax import lax
from jax.experimental import pallas as pl
from jax.experimental.pallas import tpu as pltpu
from jax.sharding import PartitionSpec as P

MESH = pl.DeviceIdType.MESH
BF16 = jnp.bfloat16
F32 = jnp.float32
NT = (((1,), (1,)), ((), ()))
TN = (((0,), (0,)), ((), ()))
NN = (((1,), (0,)), ((), ()))
NEAR = 4


def dot(a, b, dims):
    return lax.dot_general(a, b, dims, preferred_element_type=F32)


def attention_grads(query, keyval, d_attn, offset):
    rows, q_width = query.shape
    n_keys, lanes = keyval.shape
    head = lanes // 2
    scale = head**-0.5
    low = lax.broadcasted_iota(jnp.int32, (n_keys, lanes), 1) < head
    kv = keyval.astype(F32)
    vk = pltpu.roll(kv, head, 1)
    keys = jnp.concatenate(
        [jnp.where(low, kv * scale, 0.0), jnp.where(low, 0.0, vk * scale)], axis=0
    ).astype(BF16)
    values = jnp.concatenate([jnp.where(low, vk, 0.0), jnp.where(low, 0.0, kv)], axis=0).astype(BF16)

    def stacked(array):
        return jnp.concatenate(
            [array[:, p * lanes : (p + 1) * lanes] for p in range(q_width // lanes)], axis=0
        )

    query_st, d_attn_st = stacked(query), stacked(d_attn)
    scores = dot(keys, query_st, NT)
    d_share = dot(values, d_attn_st, NT)
    width = scores.shape[1]
    place = lax.broadcasted_iota(jnp.int32, (n_keys, width), 1) % rows + offset
    causal = lax.broadcasted_iota(jnp.int32, (n_keys, width), 0) <= place
    shares, d_scores = [], []
    for i in range(2):
        s = jnp.where(causal, scores[i * n_keys : (i + 1) * n_keys], -1e30)
        e = jnp.exp(s - jnp.max(s, axis=0, keepdims=True))
        p = e / jnp.sum(e, axis=0, keepdims=True)
        dp = d_share[i * n_keys : (i + 1) * n_keys]
        ds = p * (dp - jnp.sum(p * dp, axis=0, keepdims=True))
        shares.append(p.astype(BF16))
        d_scores.append(ds.astype(BF16))
    shares = jnp.concatenate(shares, axis=0)
    d_scores = jnp.concatenate(d_scores, axis=0)
    d_query_st = dot(d_scores, keys, TN).astype(BF16)
    d_query = jnp.concatenate(
        [d_query_st[p * rows : (p + 1) * rows] for p in range(q_width // lanes)], axis=1
    )
    dk = dot(d_scores, query_st, NN) * scale
    dv = dot(shares, d_attn_st, NN)
    d_keyval = jnp.where(low, dk[:n_keys], dv[n_keys:]) + pltpu.roll(
        jnp.where(low, dv[:n_keys], dk[n_keys:]), head, 1
    )
    return d_query, d_keyval


def folded(rows):
    half = rows.shape[1] // 2
    return jnp.concatenate([rows[:, :half], rows[:, half:]], axis=0)


def unfolded(rows):
    count = rows.shape[0] // 2
    return jnp.concatenate([rows[:count], rows[count:]], axis=1)


def kernel(
    n_tensor,
    n_dp,
    cot_hbm,
    xin_hbm,
    xn_hbm,
    q_hbm,
    kv_hbm,
    gain_hbm,
    wq_hbm,
    wkv_hbm,
    wo_hbm,
    out_ref,
    grad_ref,
    xin,
    xn,
    q,
    kv,
    gain,
    wq,
    wkv,
    wo,
    gathered,
    parts,
    landed,
    outs,
    final,
    cot,
    cot_folded,
    xf_out,
    xf,
    carried,
    kept,
    dkv,
    turned,
    core_out,
    core_own,
    core_in,
    z1_out,
    z1_in,
    z2_out,
    z2_in,
    load_sem,
    ag_send,
    ag_recv,
    out_send,
    rs_send,
    rs_recv,
    fin_send,
    fin_recv,
    xf_send,
    xf_recv,
    core_send,
    core_recv,
    z1_send,
    z1_recv,
    z2_send,
    z2_recv,
    go_sem,
    token_sem,
):
    s = lax.axis_index("section")
    t = lax.axis_index("tensor")
    d = lax.axis_index("dp")
    z, core = d // 2, d % 2
    n_z = n_dp // 2
    n_far = n_z // NEAR
    zi, zg = z % NEAR, z // NEAR
    shard, half_width = outs.shape[2:]
    small = shard // 2
    n_rows = q.shape[2]
    half_rows = n_rows // 2
    home = t // (n_tensor // 2)
    chunk = grad_ref.shape[1]
    first = s == 1

    n_x = n_tensor // 2
    ty, tx = t // n_x, lax.rem(t, n_x)

    def tensor_peer(j):
        return lax.rem(ty + j // n_x, 2) * n_x + lax.rem(tx + j % n_x, n_x)

    def distance(j):
        return 2 * (j // n_x) + min(j % n_x, n_x - j % n_x)

    others = sorted(range(1, n_tensor), key=lambda j: -distance(j))

    def near_peer(j):
        return (zg * NEAR + lax.rem(zi + j, NEAR)) * 2 + core

    def far_peer(j):
        return (lax.rem(zg + j, n_far) * NEAR + zi) * 2 + core

    barrier = pltpu.get_barrier_semaphore()

    def hello(device):
        pl.semaphore_signal(barrier, inc=1, device_id=device, device_id_type=MESH)

    for j in range(1, n_tensor):
        hello({"tensor": tensor_peer(j)})
    for j in range(n_tensor):
        hello({"section": 1 - s, "tensor": tensor_peer(j)})
    hello({"dp": z * 2 + 1 - core})
    for j in range(1, NEAR):
        hello({"dp": near_peer(j)})
    for j in (1, n_far - 1):
        hello({"dp": far_peer(j)})

    loads = [
        pltpu.make_async_copy(src, dst, load_sem.at[i])
        for i, (src, dst) in enumerate(
            [
                (cot_hbm, cot),
                (xin_hbm, xin),
                (wo_hbm, wo),
                (q_hbm, q),
                (kv_hbm, kv),
                (wq_hbm, wq),
                (wkv_hbm, wkv),
                (gain_hbm, gain),
                (xn_hbm, xn),
            ]
        )
    ]
    for load in loads:
        load.start()

    loads[0].wait()
    for b in range(2):
        cot_folded[b] = folded(cot[...].astype(F32)[b * small : (b + 1) * small]).astype(BF16)
    loads[1].wait()
    for i in range(4):
        rows = xin[i // 2, i % 2].astype(F32)
        for b in range(2):
            xf_out[b, i] = folded(rows[b * small : (b + 1) * small]).astype(BF16)

    pl.semaphore_wait(barrier, 2 * n_tensor - 1 + 1 + NEAR - 1 + 2)

    def rows_of(index):
        return pl.ds(pl.multiple_of(index * shard, shard), shard)

    def block_of(b):
        return 2 * lax.rem(t, n_tensor // 2) + b

    def start_copy(item, b, j, section):
        return pltpu.make_async_remote_copy(
            src_ref=cot_folded.at[b],
            dst_ref=gathered.at[item, home, rows_of(block_of(b))],
            send_sem=ag_send.at[b, j],
            recv_sem=ag_recv.at[item, home, block_of(b)],
            device_id={"section": section, "tensor": tensor_peer(j)},
            device_id_type=MESH,
        )

    def own_shard_copy(b):
        return pltpu.make_async_copy(
            cot_folded.at[b],
            gathered.at[0, home, rows_of(block_of(b))],
            ag_recv.at[0, home, block_of(b)],
        )

    def reply_copy(k, h, item, j):
        return pltpu.make_async_remote_copy(
            src_ref=outs.at[k, h],
            dst_ref=gathered.at[item, h, rows_of(t)],
            send_sem=out_send.at[k, h, j],
            recv_sem=ag_recv.at[item, h, t],
            device_id={"section": 1 - s, "tensor": lax.rem(t + j, n_tensor)},
            device_id_type=MESH,
        )

    def arrival(k, h, r):
        return pltpu.make_async_remote_copy(
            src_ref=outs.at[0, h],
            dst_ref=gathered.at[k, h, r * shard : (r + 1) * shard],
            send_sem=out_send.at[0, h, 0],
            recv_sem=ag_recv.at[k, h, r],
            device_id={"section": 1 - s},
            device_id_type=MESH,
        )

    def reduce_copy(k, h, j):
        return pltpu.make_async_remote_copy(
            src_ref=parts.at[k, h, rows_of(tensor_peer(j))],
            dst_ref=landed.at[k, h, rows_of(j)],
            send_sem=rs_send.at[k, h, j],
            recv_sem=rs_recv.at[k, h, j],
            device_id={"tensor": tensor_peer(j)},
            device_id_type=MESH,
        )

    def result_owner(h):
        return h * (n_tensor // 2) + t // 2

    def final_copy(k, h, section):
        return pltpu.make_async_remote_copy(
            src_ref=outs.at[k, h],
            dst_ref=final.at[t % 2],
            send_sem=fin_send.at[h],
            recv_sem=fin_recv.at[t % 2],
            device_id={"section": section, "tensor": result_owner(h)},
            device_id_type=MESH,
        )

    def final_last(h):
        return pltpu.make_async_remote_copy(
            src_ref=outs.at[3, h],
            dst_ref=final.at[t % 2],
            send_sem=fin_send.at[2 + h],
            recv_sem=fin_recv.at[t % 2],
            device_id={"tensor": result_owner(h)},
            device_id_type=MESH,
        )

    def final_own(k, h):
        return pltpu.make_async_copy(outs.at[k, h], final.at[t % 2], fin_recv.at[t % 2])

    def final_arrival(b):
        return pltpu.make_async_remote_copy(
            src_ref=outs.at[0, 0],
            dst_ref=final.at[b],
            send_sem=fin_send.at[0],
            recv_sem=fin_recv.at[b],
            device_id={"section": 1 - s},
            device_id_type=MESH,
        )

    def input_copy(b):
        return pltpu.make_async_remote_copy(
            src_ref=xf_out.at[b],
            dst_ref=xf.at[home],
            send_sem=xf_send.at[b],
            recv_sem=xf_recv.at[home],
            device_id={"tensor": block_of(b)},
            device_id_type=MESH,
        )

    def input_own(b):
        return pltpu.make_async_copy(xf_out.at[b], xf.at[home], xf_recv.at[home])

    def input_arrival(h):
        return pltpu.make_async_remote_copy(
            src_ref=xf_out.at[0],
            dst_ref=xf.at[h],
            send_sem=xf_send.at[0],
            recv_sem=xf_recv.at[h],
            device_id={"section": 1 - s},
            device_id_type=MESH,
        )

    def core_copy(slot):
        return pltpu.make_async_remote_copy(
            src_ref=core_out.at[slot],
            dst_ref=core_in.at[slot],
            send_sem=core_send.at[slot],
            recv_sem=core_recv.at[slot],
            device_id={"dp": z * 2 + 1 - core},
            device_id_type=MESH,
        )

    def near_copy(slot, part, j):
        span = pl.ds(part * (n_far // 2), n_far // 2)
        return pltpu.make_async_remote_copy(
            src_ref=z1_out.at[slot, lax.rem(zi + j, NEAR), span],
            dst_ref=z1_in.at[slot, j, span],
            send_sem=z1_send.at[slot, part, j],
            recv_sem=z1_recv.at[slot, part, j],
            device_id={"dp": near_peer(j)},
            device_id_type=MESH,
        )

    def far_copy(slot, j):
        return pltpu.make_async_remote_copy(
            src_ref=z2_out.at[slot, j],
            dst_ref=z2_in.at[slot, j],
            send_sem=z2_send.at[slot, j],
            recv_sem=z2_recv.at[slot, j],
            device_id={"dp": far_peer(j)},
            device_id_type=MESH,
        )

    def greet(round_index):
        for j in (1, n_far - 1):
            pl.semaphore_signal(
                token_sem.at[round_index],
                inc=1,
                device_id={"dp": far_peer(j)},
                device_id_type=MESH,
            )

    def greeted(round_index):
        pl.semaphore_wait(token_sem.at[round_index], 2)

    def turn(slot):
        def block(b, carry):
            columns = pl.ds(pl.multiple_of(b * 128, 128), 128)
            for place in range(2):
                flat = xn[slot, 1 - place, :, columns].T
                for i in range(128 // chunk):
                    owner = b * (128 // chunk) + i
                    oz, oc = owner // 2, owner % 2
                    where = (oz % NEAR) * n_far + oz // NEAR
                    turned[
                        slot,
                        oc,
                        pl.ds(pl.multiple_of(where * chunk, chunk), chunk),
                        place * n_rows : (place + 1) * n_rows,
                    ] = flat[i * chunk : (i + 1) * chunk]
            return carry

        lax.fori_loop(0, xn.shape[3] // 128, block, 0)

    def gradient(slot):
        rows = dkv[slot]

        def theirs(b, carry):
            span = pl.ds(pl.multiple_of(b * 256, 256), 256)
            core_out[slot, span] = dot(turned[slot, 1 - core, span], rows, NN).astype(BF16)
            return carry

        def ours(b, carry):
            span = pl.ds(pl.multiple_of(b * 256, 256), 256)
            core_own[slot, span] = dot(turned[slot, core, span], rows, NN)
            return carry

        count = core_out.shape[1] // 256
        lax.fori_loop(0, count, theirs, 0)
        core_copy(slot).start()
        lax.fori_loop(0, count, ours, 0)

    far_order = [(i + n_far // 4) % n_far for i in range(n_far)]

    def sum_rows(i, j):
        where = (i * n_far + lax.rem(zg + j, n_far)) * chunk
        return pl.ds(pl.multiple_of(where, chunk), chunk)

    def near_phase(slot):
        core_copy(slot).wait_recv()
        for part in range(2):
            for i in range(NEAR):
                for place in range(part * (n_far // 2), (part + 1) * (n_far // 2)):
                    span = sum_rows(i, far_order[place])
                    total = core_own[slot, span] + core_in[slot, span].astype(F32)
                    core_own[slot, span] = total
                    z1_out[slot, i, place] = total.astype(BF16)
            for j in range(1, NEAR):
                near_copy(slot, part, j).start()

    def far_phase(slot, part):
        for j in range(1, NEAR):
            near_copy(slot, part, j).wait_recv()
        places = range(part * (n_far // 2), (part + 1) * (n_far // 2))
        for place in sorted(places, key=lambda p: abs(far_order[p] - n_far // 2)):
            j = far_order[place]
            total = core_own[slot, sum_rows(zi, j)]
            for i in range(1, NEAR):
                total = total + z1_in[slot, i, place].astype(F32)
            if j:
                z2_out[slot, j] = total.astype(BF16)
                far_copy(slot, j).start()
            else:
                grad_ref[slot] = total

    def last_phase(slot):
        total = grad_ref[slot]
        for j in range(1, n_far):
            far_copy(slot, j).wait_recv()
            total = total + z2_in[slot, j].astype(F32)
        grad_ref[slot] = total

    @pl.when(first)
    def _():
        for b in range(2):
            own_shard_copy(b).start()
        for j in others:
            for b in range(2):
                start_copy(0, b, j, s).start()

    for b in range(2):

        @pl.when(block_of(b) != t)
        def _():
            input_copy(b).start()

        @pl.when(block_of(b) == t)
        def _():
            input_own(b).start()

    greet(0)
    for load in loads[2:]:
        load.wait()
    turn(1)

    @pl.when(jnp.logical_not(first))
    def _():
        pl.semaphore_wait(go_sem, 1)
        for j in range(n_tensor):
            for b in range(2):
                start_copy(1, b, j, 1 - s).start()

    def norm_half(k, h, slot, micro):
        x = xf[h, slot * 2 + micro].astype(F32)

        def over_rows(values):
            sums = jnp.sum(values, axis=-1, keepdims=True)
            mean = (sums[:small] + sums[small:]) / (2 * half_width)
            return jnp.concatenate([mean, mean], axis=0)

        r = lax.rsqrt(over_rows(x * x) + 1e-05)
        d_normed = parts[k, h, rows_of(t)].astype(F32)
        for j in range(1, n_tensor):
            reduce_copy(k, h, j).wait_recv()
            d_normed = d_normed + landed[k, h, j * shard : (j + 1) * shard].astype(F32)
        row = gain[slot]
        gains = jnp.concatenate(
            [
                jnp.broadcast_to(row[:, :half_width], (small, half_width)),
                jnp.broadcast_to(row[:, half_width:], (small, half_width)),
            ],
            axis=0,
        )
        scaled = d_normed * gains
        d_input = r * scaled - x * (r * r * r * over_rows(x * scaled))
        outs[k, h] = (gathered[k, h, rows_of(t)].astype(F32) + d_input).astype(BF16)

        @pl.when(first)
        def _():
            for j in range(n_tensor):
                reply_copy(k, h, k, j).start()

        @pl.when(jnp.logical_and(jnp.logical_not(first), k < 2))
        def _():
            for j in range(n_tensor):
                reply_copy(k, h, k + 2, j).start()

        @pl.when(jnp.logical_and(jnp.logical_not(first), k == 2))
        def _():
            final_copy(k, h, 1 - s).start()

        @pl.when(jnp.logical_and(jnp.logical_not(first), k == 3))
        def _():
            @pl.when(result_owner(h) != t)
            def _():
                final_last(h).start()

            @pl.when(result_owner(h) == t)
            def _():
                final_own(k, h).start()

    def kv_rows(h, place):
        start = place * n_rows + h * half_rows
        return pl.ds(pl.multiple_of(start, half_rows), half_rows)

    def project(k, h, slot, place):
        d_query, d_keyval = kept[h], dkv[slot, kv_rows(h, place)]
        tile = half_width // 2
        for c in range(2):
            sides = []
            for side in range(2):
                span = slice(side * half_width + c * tile, side * half_width + (c + 1) * tile)
                sides.append(dot(d_query, wq[slot, span], NT) + dot(d_keyval, wkv[slot, span], NT))
            blocks = []
            for r in range(n_tensor):
                blocks += [side[r * small : (r + 1) * small] for side in sides]
            parts[k, h, :, c * tile : (c + 1) * tile] = jnp.concatenate(blocks, axis=0).astype(BF16)

    def scatter(k, h):
        for j in others:
            reduce_copy(k, h, j).start()

    def step(k, carry):
        slot = 1 - k // 2
        place = k % 2
        micro = 1 - place
        tail = jnp.logical_and(k == 3, jnp.logical_not(first))
        for h in (1, 0):
            for r in range(n_tensor):
                arrival(k, h, r).wait_recv()
            low = dot(gathered[k, h], wo[slot, :, :half_width], NT)
            high = dot(gathered[k, h], wo[slot, :, half_width:], NT)
            d_attn = jnp.concatenate(
                [
                    low[r * shard : r * shard + small] + high[r * shard + small : (r + 1) * shard]
                    for r in range(n_tensor)
                ],
                axis=0,
            ).astype(BF16)
            base = h * half_rows
            d_query, d_keyval = attention_grads(
                q[slot, micro, base : base + half_rows],
                kv[slot, micro, : base + half_rows],
                d_attn,
                base,
            )
            if h:
                carried[...] = d_keyval[:half_rows]
                d_keyval = d_keyval[half_rows:].astype(BF16)
            else:
                d_keyval = (d_keyval + carried[...]).astype(BF16)
            dkv[slot, kv_rows(h, place)] = d_keyval
            kept[h] = d_query
            if h:

                @pl.when(jnp.logical_not(tail))
                def _():
                    project(k, 1, slot, place)
                    scatter(k, 1)

            else:

                @pl.when(tail)
                def _():
                    gradient(0)
                    project(k, 1, slot, place)
                    scatter(k, 1)

                project(k, 0, slot, place)

                @pl.when(tail)
                def _():
                    near_phase(0)

                scatter(k, 0)

        @pl.when(jnp.logical_and(first, k == 0))
        def _():
            pl.semaphore_signal(go_sem, inc=1, device_id={"section": 1 - s}, device_id_type=MESH)

        @pl.when(k == 0)
        def _():
            turn(0)
            for h in range(2):
                input_arrival(h).wait_recv()

        @pl.when(jnp.logical_and(place == 1, jnp.logical_not(tail)))
        def _():
            gradient(slot)

        @pl.when(k < 2)
        def _():
            greeted(k)
            greet(k + 1)

        @pl.when(tail)
        def _():
            far_phase(0, 0)

        norm_half(k, 1, slot, micro)

        @pl.when(tail)
        def _():
            far_phase(0, 1)

        norm_half(k, 0, slot, micro)

        @pl.when(jnp.logical_and(place == 1, jnp.logical_not(tail)))
        def _():
            near_phase(slot)

        @pl.when(k == 2)
        def _():
            greeted(2)
            far_phase(1, 0)
            far_phase(1, 1)

        return carry

    lax.fori_loop(0, 4, step, 0)

    @pl.when(first)
    def _():
        far_phase(0, 0)
        far_phase(0, 1)

    for b in range(2):
        final_arrival(b).wait_recv()
    out_ref[...] = jnp.concatenate(
        [unfolded(final[b].astype(F32)) for b in range(2)], axis=0
    ).astype(BF16)

    @pl.when(first)
    def _():
        for j in range(1, n_tensor):
            for b in range(2):
                start_copy(0, b, j, s).wait_send()
        for k in range(4):
            for h in range(2):
                for j in range(n_tensor):
                    reply_copy(k, h, k, j).wait_send()

    @pl.when(jnp.logical_not(first))
    def _():
        for j in range(n_tensor):
            for b in range(2):
                start_copy(1, b, j, 1 - s).wait_send()
        for k in range(2):
            for h in range(2):
                for j in range(n_tensor):
                    reply_copy(k, h, k + 2, j).wait_send()
        for h in range(2):
            final_copy(2, h, 1 - s).wait_send()

            @pl.when(result_owner(h) != t)
            def _():
                final_last(h).wait_send()

    for b in range(2):

        @pl.when(block_of(b) != t)
        def _():
            input_copy(b).wait_send()

    last_phase(1)
    last_phase(0)
    for k in range(4):
        for h in range(2):
            for j in range(1, n_tensor):
                reduce_copy(k, h, j).wait_send()
    for slot in range(2):
        core_copy(slot).wait_send()
        for part in range(2):
            for j in range(1, NEAR):
                near_copy(slot, part, j).wait_send()
        for j in range(1, n_far):
            far_copy(slot, j).wait_send()


def on_device(
    n_tensor,
    n_dp,
    cotangent,
    saved_input,
    saved_normed,
    saved_query,
    saved_keyval,
    norm_gain,
    w_query,
    w_keyval,
    w_output,
):
    layers, _, micros, _, shard, width = saved_input.shape
    n_rows, q_width = saved_query.shape[4:]
    kv_width = w_keyval.shape[4]
    chunk = width // n_dp
    n_z = n_dp // 2
    n_far = n_z // NEAR
    items = layers * micros
    any_spec = pl.BlockSpec(memory_space=pl.ANY)
    vmem_spec = pl.BlockSpec(memory_space=pltpu.VMEM)
    dma = pltpu.SemaphoreType.DMA
    input_grad, keyval_grad = pl.pallas_call(
        functools.partial(kernel, n_tensor, n_dp),
        out_shape=(
            jax.ShapeDtypeStruct((shard, width), BF16),
            jax.ShapeDtypeStruct((layers, chunk, kv_width), F32),
        ),
        in_specs=[any_spec] * 9,
        out_specs=(vmem_spec, vmem_spec),
        scratch_shapes=[
            pltpu.VMEM((layers, micros, shard, width), BF16),
            pltpu.VMEM((layers, micros, n_rows, width), BF16),
            pltpu.VMEM((layers, micros, n_rows, q_width), BF16),
            pltpu.VMEM((layers, micros, n_rows, kv_width), BF16),
            pltpu.VMEM((layers, 1, width), F32),
            pltpu.VMEM((layers, width, q_width), BF16),
            pltpu.VMEM((layers, width, kv_width), BF16),
            pltpu.VMEM((layers, q_width, width), BF16),
            pltpu.VMEM((items, 2, n_rows, width // 2), BF16),
            pltpu.VMEM((items, 2, n_rows, width // 2), BF16),
            pltpu.VMEM((items, 2, n_rows, width // 2), BF16),
            pltpu.VMEM((items, 2, shard, width // 2), BF16),
            pltpu.VMEM((2, shard, width // 2), BF16),
            pltpu.VMEM((shard, width), BF16),
            pltpu.VMEM((2, shard, width // 2), BF16),
            pltpu.VMEM((2, items, shard, width // 2), BF16),
            pltpu.VMEM((2, items, shard, width // 2), BF16),
            pltpu.VMEM((n_rows // 2, kv_width), F32),
            pltpu.VMEM((2, n_rows // 2, q_width), BF16),
            pltpu.VMEM((layers, micros * n_rows, kv_width), BF16),
            pltpu.VMEM((layers, 2, width // 2, micros * n_rows), BF16),
            pltpu.VMEM((layers, width // 2, kv_width), BF16),
            pltpu.VMEM((layers, width // 2, kv_width), F32),
            pltpu.VMEM((layers, width // 2, kv_width), BF16),
            pltpu.VMEM((layers, NEAR, n_far, chunk, kv_width), BF16),
            pltpu.VMEM((layers, NEAR, n_far, chunk, kv_width), BF16),
            pltpu.VMEM((layers, n_far, chunk, kv_width), BF16),
            pltpu.VMEM((layers, n_far, chunk, kv_width), BF16),
            dma((9,)),
            dma((2, n_tensor)),
            dma((items, 2, n_tensor)),
            dma((items, 2, n_tensor)),
            dma((items, 2, n_tensor)),
            dma((items, 2, n_tensor)),
            dma((4,)),
            dma((2,)),
            dma((2,)),
            dma((2,)),
            dma((layers,)),
            dma((layers,)),
            dma((layers, 2, NEAR)),
            dma((layers, 2, NEAR)),
            dma((layers, n_far)),
            dma((layers, n_far)),
            pltpu.SemaphoreType.REGULAR,
            pltpu.SemaphoreType.REGULAR((3,)),
        ],
        compiler_params=pltpu.CompilerParams(
            collective_id=0, has_side_effects=True, vmem_limit_bytes=56 * 2**20
        ),
        name="backward",
    )(
        cotangent.reshape(shard, width),
        saved_input.reshape(layers, micros, shard, width),
        saved_normed.reshape(layers, micros, n_rows, width),
        saved_query.reshape(layers, micros, n_rows, q_width),
        saved_keyval.reshape(layers, micros, n_rows, kv_width),
        norm_gain,
        w_query.reshape(layers, width, q_width),
        w_keyval.reshape(layers, width, kv_width),
        w_output.reshape(layers, q_width, width),
    )
    return (
        input_grad[None, None],
        keyval_grad.reshape(layers, 1, chunk, 1, kv_width),
    )


def solution(mesh):
    in_specs = (
        P("section", "dp", "tensor", None),
        P(None, "section", None, "dp", "tensor", None),
        P(None, "section", None, "dp", None, None),
        P(None, "section", None, "dp", None, "tensor"),
        P(None, "section", None, "dp", None, "tensor", None),
        P(None, "section", None),
        P(None, "section", None, "tensor"),
        P(None, "section", None, "tensor", None),
        P(None, "section", "tensor", None),
    )
    out_specs = (P("section", "dp", "tensor", None), P(None, "section", "dp", "tensor", None))
    return jax.shard_map(
        functools.partial(on_device, mesh.shape["tensor"], mesh.shape["dp"]),
        mesh=mesh,
        in_specs=in_specs,
        out_specs=out_specs,
        check_vma=False,
    )
```

```python
import functools

import jax
import jax.numpy as jnp
from jax import lax
from jax.experimental import pallas as pl
from jax.experimental.pallas import tpu as pltpu
from jax.sharding import PartitionSpec as P

MESH = pl.DeviceIdType.MESH
BF16 = jnp.bfloat16
F32 = jnp.float32
NT = (((1,), (1,)), ((), ()))
TN = (((0,), (0,)), ((), ()))
NN = (((1,), (0,)), ((), ()))
NEAR = 4


def dot(a, b, dims):
    return lax.dot_general(a, b, dims, preferred_element_type=F32)


def padded(keyval):
    n_keys, lanes = keyval.shape
    head = lanes // 2
    low = lax.broadcasted_iota(jnp.int32, (n_keys, lanes), 1) < head
    kv = keyval.astype(F32)
    vk = pltpu.roll(kv, head, 1)
    keys = jnp.concatenate(
        [jnp.where(low, kv * head**-0.5, 0.0), jnp.where(low, 0.0, vk * head**-0.5)], axis=0
    ).astype(BF16)
    values = jnp.concatenate([jnp.where(low, vk, 0.0), jnp.where(low, 0.0, kv)], axis=0).astype(BF16)
    return keys, values, low


def stacked(array, lanes):
    return jnp.concatenate(
        [array[:, p * lanes : (p + 1) * lanes] for p in range(array.shape[1] // lanes)], axis=0
    )


def attention_shares(query, keyval, offset):
    rows = query.shape[0]
    n_keys, lanes = keyval.shape
    keys, _, _ = padded(keyval)
    scores = dot(keys, stacked(query, lanes), NT)
    width = scores.shape[1]
    place = lax.broadcasted_iota(jnp.int32, (n_keys, width), 1) % rows + offset
    causal = lax.broadcasted_iota(jnp.int32, (n_keys, width), 0) <= place
    shares = []
    for i in range(2):
        s = jnp.where(causal, scores[i * n_keys : (i + 1) * n_keys], -1e30)
        e = jnp.exp(s - jnp.max(s, axis=0, keepdims=True))
        shares.append(e / jnp.sum(e, axis=0, keepdims=True))
    return jnp.concatenate(shares, axis=0)


def attention_grads(query, keyval, d_attn, shares):
    rows, q_width = query.shape
    n_keys, lanes = keyval.shape
    head = lanes // 2
    keys, values, low = padded(keyval)
    query_st, d_attn_st = stacked(query, lanes), stacked(d_attn, lanes)
    d_share = dot(values, d_attn_st, NT)
    d_scores = []
    for i in range(2):
        p = shares[i * n_keys : (i + 1) * n_keys]
        dp = d_share[i * n_keys : (i + 1) * n_keys]
        d_scores.append((p * (dp - jnp.sum(p * dp, axis=0, keepdims=True))).astype(BF16))
    d_scores = jnp.concatenate(d_scores, axis=0)
    d_query_st = dot(d_scores, keys, TN).astype(BF16)
    d_query = jnp.concatenate(
        [d_query_st[p * rows : (p + 1) * rows] for p in range(q_width // lanes)], axis=1
    )
    dk = dot(d_scores, query_st, NN) * head**-0.5
    dv = dot(shares.astype(BF16), d_attn_st, NN)
    d_keyval = jnp.where(low, dk[:n_keys], dv[n_keys:]) + pltpu.roll(
        jnp.where(low, dv[:n_keys], dk[n_keys:]), head, 1
    )
    return d_query, d_keyval


def folded(rows):
    half = rows.shape[1] // 2
    return jnp.concatenate([rows[:, :half], rows[:, half:]], axis=0)


def unfolded(rows):
    count = rows.shape[0] // 2
    return jnp.concatenate([rows[:count], rows[count:]], axis=1)


def kernel(
    n_tensor,
    n_dp,
    cot_hbm,
    xin_hbm,
    xn_hbm,
    q_hbm,
    kv_hbm,
    gain_hbm,
    wq_hbm,
    wkv_hbm,
    wo_hbm,
    out_ref,
    grad_ref,
    xin,
    xn,
    q,
    kv,
    gain,
    wq,
    wkv,
    wo,
    gathered,
    parts,
    landed,
    outs,
    final,
    cot,
    cot_folded,
    xf_out,
    xf,
    carried,
    kept,
    shares,
    dkv,
    turned,
    core_out,
    core_own,
    core_in,
    z1_out,
    z1_in,
    z2_out,
    z2_in,
    load_sem,
    ag_send,
    ag_recv,
    out_send,
    rs_send,
    rs_recv,
    fin_send,
    fin_recv,
    xf_send,
    xf_recv,
    core_send,
    core_recv,
    z1_send,
    z1_recv,
    z2_send,
    z2_recv,
    go_sem,
    token_sem,
):
    s = lax.axis_index("section")
    t = lax.axis_index("tensor")
    d = lax.axis_index("dp")
    z, core = d // 2, d % 2
    n_z = n_dp // 2
    n_far = n_z // NEAR
    zi, zg = z % NEAR, z // NEAR
    shard, half_width = outs.shape[2:]
    small = shard // 2
    n_rows = q.shape[2]
    half_rows = n_rows // 2
    home = t // (n_tensor // 2)
    chunk = grad_ref.shape[1]
    first = s == 1

    n_x = n_tensor // 2
    ty, tx = t // n_x, lax.rem(t, n_x)

    def tensor_peer(j):
        return lax.rem(ty + j // n_x, 2) * n_x + lax.rem(tx + j % n_x, n_x)

    def distance(j):
        return 2 * (j // n_x) + min(j % n_x, n_x - j % n_x)

    others = sorted(range(1, n_tensor), key=lambda j: -distance(j))

    def near_peer(j):
        return (zg * NEAR + lax.rem(zi + j, NEAR)) * 2 + core

    def far_peer(j):
        return (lax.rem(zg + j, n_far) * NEAR + zi) * 2 + core

    barrier = pltpu.get_barrier_semaphore()

    def hello(device):
        pl.semaphore_signal(barrier, inc=1, device_id=device, device_id_type=MESH)

    for j in range(1, n_tensor):
        hello({"tensor": tensor_peer(j)})
    for j in range(n_tensor):
        hello({"section": 1 - s, "tensor": tensor_peer(j)})
    hello({"dp": z * 2 + 1 - core})
    for j in range(1, NEAR):
        hello({"dp": near_peer(j)})
    for j in (1, n_far - 1):
        hello({"dp": far_peer(j)})

    loads = [
        pltpu.make_async_copy(src, dst, load_sem.at[i])
        for i, (src, dst) in enumerate(
            [
                (cot_hbm, cot),
                (xin_hbm, xin),
                (wo_hbm, wo),
                (q_hbm, q),
                (kv_hbm, kv),
                (wq_hbm, wq),
                (wkv_hbm, wkv),
                (gain_hbm, gain),
                (xn_hbm, xn),
            ]
        )
    ]
    for load in loads:
        load.start()

    loads[0].wait()
    for b in range(2):
        cot_folded[b] = folded(cot[...].astype(F32)[b * small : (b + 1) * small]).astype(BF16)
    loads[1].wait()
    for i in range(4):
        rows = xin[i // 2, i % 2].astype(F32)
        for b in range(2):
            xf_out[b, i] = folded(rows[b * small : (b + 1) * small]).astype(BF16)

    pl.semaphore_wait(barrier, 2 * n_tensor - 1 + 1 + NEAR - 1 + 2)

    def rows_of(index):
        return pl.ds(pl.multiple_of(index * shard, shard), shard)

    def block_of(b):
        return 2 * lax.rem(t, n_tensor // 2) + b

    def start_copy(item, b, j, section):
        return pltpu.make_async_remote_copy(
            src_ref=cot_folded.at[b],
            dst_ref=gathered.at[item, home, rows_of(block_of(b))],
            send_sem=ag_send.at[b, j],
            recv_sem=ag_recv.at[item, home, block_of(b)],
            device_id={"section": section, "tensor": tensor_peer(j)},
            device_id_type=MESH,
        )

    def own_shard_copy(b):
        return pltpu.make_async_copy(
            cot_folded.at[b],
            gathered.at[0, home, rows_of(block_of(b))],
            ag_recv.at[0, home, block_of(b)],
        )

    def reply_copy(k, h, item, j):
        return pltpu.make_async_remote_copy(
            src_ref=outs.at[k, h],
            dst_ref=gathered.at[item, h, rows_of(t)],
            send_sem=out_send.at[k, h, j],
            recv_sem=ag_recv.at[item, h, t],
            device_id={"section": 1 - s, "tensor": lax.rem(t + j, n_tensor)},
            device_id_type=MESH,
        )

    def arrival(k, h, r):
        return pltpu.make_async_remote_copy(
            src_ref=outs.at[0, h],
            dst_ref=gathered.at[k, h, r * shard : (r + 1) * shard],
            send_sem=out_send.at[0, h, 0],
            recv_sem=ag_recv.at[k, h, r],
            device_id={"section": 1 - s},
            device_id_type=MESH,
        )

    def reduce_copy(k, h, c, j):
        span = pl.ds(c * (half_width // 2), half_width // 2)
        return pltpu.make_async_remote_copy(
            src_ref=parts.at[k, h, rows_of(tensor_peer(j)), span],
            dst_ref=landed.at[k, h, rows_of(j), span],
            send_sem=rs_send.at[k, h, c, j],
            recv_sem=rs_recv.at[k, h, c, j],
            device_id={"tensor": tensor_peer(j)},
            device_id_type=MESH,
        )

    def result_owner(h):
        return h * (n_tensor // 2) + t // 2

    def final_copy(k, h, section):
        return pltpu.make_async_remote_copy(
            src_ref=outs.at[k, h],
            dst_ref=final.at[t % 2],
            send_sem=fin_send.at[h],
            recv_sem=fin_recv.at[t % 2],
            device_id={"section": section, "tensor": result_owner(h)},
            device_id_type=MESH,
        )

    def final_last(h):
        return pltpu.make_async_remote_copy(
            src_ref=outs.at[3, h],
            dst_ref=final.at[t % 2],
            send_sem=fin_send.at[2 + h],
            recv_sem=fin_recv.at[t % 2],
            device_id={"tensor": result_owner(h)},
            device_id_type=MESH,
        )

    def final_own(k, h):
        return pltpu.make_async_copy(outs.at[k, h], final.at[t % 2], fin_recv.at[t % 2])

    def final_arrival(b):
        return pltpu.make_async_remote_copy(
            src_ref=outs.at[0, 0],
            dst_ref=final.at[b],
            send_sem=fin_send.at[0],
            recv_sem=fin_recv.at[b],
            device_id={"section": 1 - s},
            device_id_type=MESH,
        )

    def input_copy(b):
        return pltpu.make_async_remote_copy(
            src_ref=xf_out.at[b],
            dst_ref=xf.at[home],
            send_sem=xf_send.at[b],
            recv_sem=xf_recv.at[home],
            device_id={"tensor": block_of(b)},
            device_id_type=MESH,
        )

    def input_own(b):
        return pltpu.make_async_copy(xf_out.at[b], xf.at[home], xf_recv.at[home])

    def input_arrival(h):
        return pltpu.make_async_remote_copy(
            src_ref=xf_out.at[0],
            dst_ref=xf.at[h],
            send_sem=xf_send.at[0],
            recv_sem=xf_recv.at[h],
            device_id={"section": 1 - s},
            device_id_type=MESH,
        )

    def core_copy(slot):
        return pltpu.make_async_remote_copy(
            src_ref=core_out.at[slot],
            dst_ref=core_in.at[slot],
            send_sem=core_send.at[slot],
            recv_sem=core_recv.at[slot],
            device_id={"dp": z * 2 + 1 - core},
            device_id_type=MESH,
        )

    def near_copy(slot, part, j):
        span = pl.ds(part * (n_far // 2), n_far // 2)
        return pltpu.make_async_remote_copy(
            src_ref=z1_out.at[slot, lax.rem(zi + j, NEAR), span],
            dst_ref=z1_in.at[slot, j, span],
            send_sem=z1_send.at[slot, part, j],
            recv_sem=z1_recv.at[slot, part, j],
            device_id={"dp": near_peer(j)},
            device_id_type=MESH,
        )

    def far_copy(slot, j):
        return pltpu.make_async_remote_copy(
            src_ref=z2_out.at[slot, j],
            dst_ref=z2_in.at[slot, j],
            send_sem=z2_send.at[slot, j],
            recv_sem=z2_recv.at[slot, j],
            device_id={"dp": far_peer(j)},
            device_id_type=MESH,
        )

    def greet(round_index):
        for j in (1, n_far - 1):
            pl.semaphore_signal(
                token_sem.at[round_index],
                inc=1,
                device_id={"dp": far_peer(j)},
                device_id_type=MESH,
            )

    def greeted(round_index):
        pl.semaphore_wait(token_sem.at[round_index], 2)

    def turn(slot):
        def block(b, carry):
            columns = pl.ds(pl.multiple_of(b * 128, 128), 128)
            for place in range(2):
                flat = xn[slot, 1 - place, :, columns].T
                for i in range(128 // chunk):
                    owner = b * (128 // chunk) + i
                    oz, oc = owner // 2, owner % 2
                    where = (oz % NEAR) * n_far + oz // NEAR
                    turned[
                        slot,
                        oc,
                        pl.ds(pl.multiple_of(where * chunk, chunk), chunk),
                        place * n_rows : (place + 1) * n_rows,
                    ] = flat[i * chunk : (i + 1) * chunk]
            return carry

        lax.fori_loop(0, xn.shape[3] // 128, block, 0)

    def gradient(slot):
        rows = dkv[slot]

        def theirs(b, carry):
            span = pl.ds(pl.multiple_of(b * 256, 256), 256)
            core_out[slot, span] = dot(turned[slot, 1 - core, span], rows, NN).astype(BF16)
            return carry

        def ours(b, carry):
            span = pl.ds(pl.multiple_of(b * 256, 256), 256)
            core_own[slot, span] = dot(turned[slot, core, span], rows, NN)
            return carry

        count = core_out.shape[1] // 256
        lax.fori_loop(0, count, theirs, 0)
        core_copy(slot).start()
        lax.fori_loop(0, count, ours, 0)

    far_order = [(i + n_far // 4) % n_far for i in range(n_far)]

    def sum_rows(i, j):
        where = (i * n_far + lax.rem(zg + j, n_far)) * chunk
        return pl.ds(pl.multiple_of(where, chunk), chunk)

    def near_phase(slot):
        core_copy(slot).wait_recv()
        for part in range(2):
            for i in range(NEAR):
                for place in range(part * (n_far // 2), (part + 1) * (n_far // 2)):
                    span = sum_rows(i, far_order[place])
                    total = core_own[slot, span] + core_in[slot, span].astype(F32)
                    core_own[slot, span] = total
                    z1_out[slot, i, place] = total.astype(BF16)
            for j in range(1, NEAR):
                near_copy(slot, part, j).start()

    def far_phase(slot, part):
        for j in range(1, NEAR):
            near_copy(slot, part, j).wait_recv()
        places = range(part * (n_far // 2), (part + 1) * (n_far // 2))
        for place in sorted(places, key=lambda p: abs(far_order[p] - n_far // 2)):
            j = far_order[place]
            total = core_own[slot, sum_rows(zi, j)]
            for i in range(1, NEAR):
                total = total + z1_in[slot, i, place].astype(F32)
            if j:
                z2_out[slot, j] = total.astype(BF16)
                far_copy(slot, j).start()
            else:
                grad_ref[slot] = total

    def last_phase(slot):
        total = grad_ref[slot]
        for j in range(1, n_far):
            far_copy(slot, j).wait_recv()
            total = total + z2_in[slot, j].astype(F32)
        grad_ref[slot] = total

    @pl.when(first)
    def _():
        for b in range(2):
            own_shard_copy(b).start()
        for j in others:
            for b in range(2):
                start_copy(0, b, j, s).start()

    for b in range(2):

        @pl.when(block_of(b) != t)
        def _():
            input_copy(b).start()

        @pl.when(block_of(b) == t)
        def _():
            input_own(b).start()

    greet(0)
    for load in loads[2:]:
        load.wait()
    turn(1)

    @pl.when(jnp.logical_not(first))
    def _():
        pl.semaphore_wait(go_sem, 1)
        for j in range(n_tensor):
            for b in range(2):
                start_copy(1, b, j, 1 - s).start()

    def norm_half(k, h, slot, micro):
        x = xf[h, slot * 2 + micro].astype(F32)

        def over_rows(values):
            sums = jnp.sum(values, axis=-1, keepdims=True)
            mean = (sums[:small] + sums[small:]) / (2 * half_width)
            return jnp.concatenate([mean, mean], axis=0)

        r = lax.rsqrt(over_rows(x * x) + 1e-05)
        d_normed = parts[k, h, rows_of(t)].astype(F32)
        for j in range(1, n_tensor):
            for c in range(2):
                reduce_copy(k, h, c, j).wait_recv()
            d_normed = d_normed + landed[k, h, j * shard : (j + 1) * shard].astype(F32)
        row = gain[slot]
        gains = jnp.concatenate(
            [
                jnp.broadcast_to(row[:, :half_width], (small, half_width)),
                jnp.broadcast_to(row[:, half_width:], (small, half_width)),
            ],
            axis=0,
        )
        scaled = d_normed * gains
        d_input = r * scaled - x * (r * r * r * over_rows(x * scaled))
        outs[k, h] = (gathered[k, h, rows_of(t)].astype(F32) + d_input).astype(BF16)

        @pl.when(first)
        def _():
            for j in range(n_tensor):
                reply_copy(k, h, k, j).start()

        @pl.when(jnp.logical_and(jnp.logical_not(first), k < 2))
        def _():
            for j in range(n_tensor):
                reply_copy(k, h, k + 2, j).start()

        @pl.when(jnp.logical_and(jnp.logical_not(first), k == 2))
        def _():
            final_copy(k, h, 1 - s).start()

        @pl.when(jnp.logical_and(jnp.logical_not(first), k == 3))
        def _():
            @pl.when(result_owner(h) != t)
            def _():
                final_last(h).start()

            @pl.when(result_owner(h) == t)
            def _():
                final_own(k, h).start()

    def kv_rows(h, place):
        start = place * n_rows + h * half_rows
        return pl.ds(pl.multiple_of(start, half_rows), half_rows)

    def project(k, h, slot, place):
        d_query, d_keyval = kept[h], dkv[slot, kv_rows(h, place)]
        tile = half_width // 2
        for c in range(2):
            sides = []
            for side in range(2):
                span = slice(side * half_width + c * tile, side * half_width + (c + 1) * tile)
                sides.append(dot(d_query, wq[slot, span], NT) + dot(d_keyval, wkv[slot, span], NT))
            blocks = []
            for r in range(n_tensor):
                blocks += [side[r * small : (r + 1) * small] for side in sides]
            parts[k, h, :, c * tile : (c + 1) * tile] = jnp.concatenate(blocks, axis=0).astype(BF16)
            for j in others:
                reduce_copy(k, h, c, j).start()

    def prepare(k):
        slot, micro = 1 - k // 2, 1 - k % 2
        for h in range(2):
            base = h * half_rows
            shares[h, : 2 * (base + half_rows)] = attention_shares(
                q[slot, micro, base : base + half_rows], kv[slot, micro, : base + half_rows], base
            )

    def step(k, carry):
        slot = 1 - k // 2
        place = k % 2
        micro = 1 - place
        tail = jnp.logical_and(k == 3, jnp.logical_not(first))
        for h in (1, 0):
            for r in range(n_tensor):
                arrival(k, h, r).wait_recv()
            low = dot(gathered[k, h], wo[slot, :, :half_width], NT)
            high = dot(gathered[k, h], wo[slot, :, half_width:], NT)
            d_attn = jnp.concatenate(
                [
                    low[r * shard : r * shard + small] + high[r * shard + small : (r + 1) * shard]
                    for r in range(n_tensor)
                ],
                axis=0,
            ).astype(BF16)
            base = h * half_rows
            d_query, d_keyval = attention_grads(
                q[slot, micro, base : base + half_rows],
                kv[slot, micro, : base + half_rows],
                d_attn,
                shares[h, : 2 * (base + half_rows)],
            )
            if h:
                carried[...] = d_keyval[:half_rows]
                d_keyval = d_keyval[half_rows:].astype(BF16)
            else:
                d_keyval = (d_keyval + carried[...]).astype(BF16)
            dkv[slot, kv_rows(h, place)] = d_keyval
            kept[h] = d_query
            if h:

                @pl.when(jnp.logical_not(tail))
                def _():
                    project(k, 1, slot, place)

            else:

                @pl.when(tail)
                def _():
                    gradient(0)
                    project(k, 1, slot, place)

                project(k, 0, slot, place)

                @pl.when(tail)
                def _():
                    near_phase(0)

        @pl.when(jnp.logical_and(first, k == 0))
        def _():
            pl.semaphore_signal(go_sem, inc=1, device_id={"section": 1 - s}, device_id_type=MESH)

        @pl.when(k == 0)
        def _():
            turn(0)
            for h in range(2):
                input_arrival(h).wait_recv()

        @pl.when(jnp.logical_and(place == 1, jnp.logical_not(tail)))
        def _():
            gradient(slot)

        @pl.when(k < 2)
        def _():
            greeted(k)
            greet(k + 1)

        @pl.when(k < 3)
        def _():
            prepare(k + 1)

        @pl.when(tail)
        def _():
            far_phase(0, 0)

        norm_half(k, 1, slot, micro)

        @pl.when(tail)
        def _():
            far_phase(0, 1)

        norm_half(k, 0, slot, micro)

        @pl.when(jnp.logical_and(place == 1, jnp.logical_not(tail)))
        def _():
            near_phase(slot)

        @pl.when(k == 2)
        def _():
            greeted(2)
            far_phase(1, 0)
            far_phase(1, 1)

        return carry

    prepare(0)
    lax.fori_loop(0, 4, step, 0)

    @pl.when(first)
    def _():
        far_phase(0, 0)
        far_phase(0, 1)

    for b in range(2):
        final_arrival(b).wait_recv()
    out_ref[...] = jnp.concatenate(
        [unfolded(final[b].astype(F32)) for b in range(2)], axis=0
    ).astype(BF16)

    @pl.when(first)
    def _():
        for j in range(1, n_tensor):
            for b in range(2):
                start_copy(0, b, j, s).wait_send()
        for k in range(4):
            for h in range(2):
                for j in range(n_tensor):
                    reply_copy(k, h, k, j).wait_send()

    @pl.when(jnp.logical_not(first))
    def _():
        for j in range(n_tensor):
            for b in range(2):
                start_copy(1, b, j, 1 - s).wait_send()
        for k in range(2):
            for h in range(2):
                for j in range(n_tensor):
                    reply_copy(k, h, k + 2, j).wait_send()
        for h in range(2):
            final_copy(2, h, 1 - s).wait_send()

            @pl.when(result_owner(h) != t)
            def _():
                final_last(h).wait_send()

    for b in range(2):

        @pl.when(block_of(b) != t)
        def _():
            input_copy(b).wait_send()

    last_phase(1)
    last_phase(0)
    for k in range(4):
        for h in range(2):
            for c in range(2):
                for j in range(1, n_tensor):
                    reduce_copy(k, h, c, j).wait_send()
    for slot in range(2):
        core_copy(slot).wait_send()
        for part in range(2):
            for j in range(1, NEAR):
                near_copy(slot, part, j).wait_send()
        for j in range(1, n_far):
            far_copy(slot, j).wait_send()


def on_device(
    n_tensor,
    n_dp,
    cotangent,
    saved_input,
    saved_normed,
    saved_query,
    saved_keyval,
    norm_gain,
    w_query,
    w_keyval,
    w_output,
):
    layers, _, micros, _, shard, width = saved_input.shape
    n_rows, q_width = saved_query.shape[4:]
    kv_width = w_keyval.shape[4]
    chunk = width // n_dp
    n_z = n_dp // 2
    n_far = n_z // NEAR
    items = layers * micros
    any_spec = pl.BlockSpec(memory_space=pl.ANY)
    vmem_spec = pl.BlockSpec(memory_space=pltpu.VMEM)
    dma = pltpu.SemaphoreType.DMA
    input_grad, keyval_grad = pl.pallas_call(
        functools.partial(kernel, n_tensor, n_dp),
        out_shape=(
            jax.ShapeDtypeStruct((shard, width), BF16),
            jax.ShapeDtypeStruct((layers, chunk, kv_width), F32),
        ),
        in_specs=[any_spec] * 9,
        out_specs=(vmem_spec, vmem_spec),
        scratch_shapes=[
            pltpu.VMEM((layers, micros, shard, width), BF16),
            pltpu.VMEM((layers, micros, n_rows, width), BF16),
            pltpu.VMEM((layers, micros, n_rows, q_width), BF16),
            pltpu.VMEM((layers, micros, n_rows, kv_width), BF16),
            pltpu.VMEM((layers, 1, width), F32),
            pltpu.VMEM((layers, width, q_width), BF16),
            pltpu.VMEM((layers, width, kv_width), BF16),
            pltpu.VMEM((layers, q_width, width), BF16),
            pltpu.VMEM((items, 2, n_rows, width // 2), BF16),
            pltpu.VMEM((items, 2, n_rows, width // 2), BF16),
            pltpu.VMEM((items, 2, n_rows, width // 2), BF16),
            pltpu.VMEM((items, 2, shard, width // 2), BF16),
            pltpu.VMEM((2, shard, width // 2), BF16),
            pltpu.VMEM((shard, width), BF16),
            pltpu.VMEM((2, shard, width // 2), BF16),
            pltpu.VMEM((2, items, shard, width // 2), BF16),
            pltpu.VMEM((2, items, shard, width // 2), BF16),
            pltpu.VMEM((n_rows // 2, kv_width), F32),
            pltpu.VMEM((2, n_rows // 2, q_width), BF16),
            pltpu.VMEM((2, 2 * n_rows, q_width // 2), F32),
            pltpu.VMEM((layers, micros * n_rows, kv_width), BF16),
            pltpu.VMEM((layers, 2, width // 2, micros * n_rows), BF16),
            pltpu.VMEM((layers, width // 2, kv_width), BF16),
            pltpu.VMEM((layers, width // 2, kv_width), F32),
            pltpu.VMEM((layers, width // 2, kv_width), BF16),
            pltpu.VMEM((layers, NEAR, n_far, chunk, kv_width), BF16),
            pltpu.VMEM((layers, NEAR, n_far, chunk, kv_width), BF16),
            pltpu.VMEM((layers, n_far, chunk, kv_width), BF16),
            pltpu.VMEM((layers, n_far, chunk, kv_width), BF16),
            dma((9,)),
            dma((2, n_tensor)),
            dma((items, 2, n_tensor)),
            dma((items, 2, n_tensor)),
            dma((items, 2, 2, n_tensor)),
            dma((items, 2, 2, n_tensor)),
            dma((4,)),
            dma((2,)),
            dma((2,)),
            dma((2,)),
            dma((layers,)),
            dma((layers,)),
            dma((layers, 2, NEAR)),
            dma((layers, 2, NEAR)),
            dma((layers, n_far)),
            dma((layers, n_far)),
            pltpu.SemaphoreType.REGULAR,
            pltpu.SemaphoreType.REGULAR((3,)),
        ],
        compiler_params=pltpu.CompilerParams(
            collective_id=0, has_side_effects=True, vmem_limit_bytes=56 * 2**20
        ),
        name="backward",
    )(
        cotangent.reshape(shard, width),
        saved_input.reshape(layers, micros, shard, width),
        saved_normed.reshape(layers, micros, n_rows, width),
        saved_query.reshape(layers, micros, n_rows, q_width),
        saved_keyval.reshape(layers, micros, n_rows, kv_width),
        norm_gain,
        w_query.reshape(layers, width, q_width),
        w_keyval.reshape(layers, width, kv_width),
        w_output.reshape(layers, q_width, width),
    )
    return (
        input_grad[None, None],
        keyval_grad.reshape(layers, 1, chunk, 1, kv_width),
    )


def solution(mesh):
    in_specs = (
        P("section", "dp", "tensor", None),
        P(None, "section", None, "dp", "tensor", None),
        P(None, "section", None, "dp", None, None),
        P(None, "section", None, "dp", None, "tensor"),
        P(None, "section", None, "dp", None, "tensor", None),
        P(None, "section", None),
        P(None, "section", None, "tensor"),
        P(None, "section", None, "tensor", None),
        P(None, "section", "tensor", None),
    )
    out_specs = (P("section", "dp", "tensor", None), P(None, "section", "dp", "tensor", None))
    return jax.shard_map(
        functools.partial(on_device, mesh.shape["tensor"], mesh.shape["dp"]),
        mesh=mesh,
        in_specs=in_specs,
        out_specs=out_specs,
        check_vma=False,
    )
```

```python
import functools

import jax
import jax.numpy as jnp
from jax import lax
from jax.experimental import pallas as pl
from jax.experimental.pallas import tpu as pltpu
from jax.sharding import PartitionSpec as P

MESH = pl.DeviceIdType.MESH
BF16 = jnp.bfloat16
F32 = jnp.float32
NT = (((1,), (1,)), ((), ()))
TN = (((0,), (0,)), ((), ()))
NN = (((1,), (0,)), ((), ()))
NEAR = 4


def dot(a, b, dims):
    return lax.dot_general(a, b, dims, preferred_element_type=F32)


def padded(keyval):
    n_keys, lanes = keyval.shape
    head = lanes // 2
    low = lax.broadcasted_iota(jnp.int32, (n_keys, lanes), 1) < head
    kv = keyval.astype(F32)
    vk = pltpu.roll(kv, head, 1)
    keys = jnp.concatenate(
        [jnp.where(low, kv * head**-0.5, 0.0), jnp.where(low, 0.0, vk * head**-0.5)], axis=0
    ).astype(BF16)
    values = jnp.concatenate([jnp.where(low, vk, 0.0), jnp.where(low, 0.0, kv)], axis=0).astype(BF16)
    return keys, values, low


def stacked(array, lanes):
    return jnp.concatenate(
        [array[:, p * lanes : (p + 1) * lanes] for p in range(array.shape[1] // lanes)], axis=0
    )


def attention_shares(query, keyval, offset):
    rows = query.shape[0]
    n_keys, lanes = keyval.shape
    keys, _, _ = padded(keyval)
    scores = dot(keys, stacked(query, lanes), NT)
    width = scores.shape[1]
    place = lax.broadcasted_iota(jnp.int32, (n_keys, width), 1) % rows + offset
    causal = lax.broadcasted_iota(jnp.int32, (n_keys, width), 0) <= place
    shares = []
    for i in range(2):
        s = jnp.where(causal, scores[i * n_keys : (i + 1) * n_keys], -1e30)
        e = jnp.exp(s - jnp.max(s, axis=0, keepdims=True))
        shares.append(e / jnp.sum(e, axis=0, keepdims=True))
    return jnp.concatenate(shares, axis=0)


def attention_grads(query, keyval, d_attn, shares):
    rows, q_width = query.shape
    n_keys, lanes = keyval.shape
    head = lanes // 2
    keys, values, low = padded(keyval)
    query_st, d_attn_st = stacked(query, lanes), stacked(d_attn, lanes)
    d_share = dot(values, d_attn_st, NT)
    d_scores = []
    for i in range(2):
        p = shares[i * n_keys : (i + 1) * n_keys]
        dp = d_share[i * n_keys : (i + 1) * n_keys]
        d_scores.append((p * (dp - jnp.sum(p * dp, axis=0, keepdims=True))).astype(BF16))
    d_scores = jnp.concatenate(d_scores, axis=0)
    d_query_st = dot(d_scores, keys, TN).astype(BF16)
    d_query = jnp.concatenate(
        [d_query_st[p * rows : (p + 1) * rows] for p in range(q_width // lanes)], axis=1
    )
    dk = dot(d_scores, query_st, NN) * head**-0.5
    dv = dot(shares.astype(BF16), d_attn_st, NN)
    d_keyval = jnp.where(low, dk[:n_keys], dv[n_keys:]) + pltpu.roll(
        jnp.where(low, dv[:n_keys], dk[n_keys:]), head, 1
    )
    return d_query, d_keyval


def folded(rows):
    half = rows.shape[1] // 2
    return jnp.concatenate([rows[:, :half], rows[:, half:]], axis=0)


def unfolded(rows):
    count = rows.shape[0] // 2
    return jnp.concatenate([rows[:count], rows[count:]], axis=1)


def kernel(
    n_tensor,
    n_dp,
    cot_hbm,
    xin_hbm,
    xn_hbm,
    q_hbm,
    kv_hbm,
    gain_hbm,
    wq_hbm,
    wkv_hbm,
    wo_hbm,
    out_ref,
    grad_ref,
    xin,
    xn,
    q,
    kv,
    gain,
    wq,
    wkv,
    wo,
    gathered,
    parts,
    landed,
    outs,
    final,
    cot,
    cot_folded,
    xf_out,
    xf,
    carried,
    kept,
    shares,
    dkv,
    turned,
    core_out,
    core_own,
    core_in,
    z1_out,
    z1_in,
    z2_out,
    z2_in,
    load_sem,
    ag_send,
    ag_recv,
    out_send,
    rs_send,
    rs_recv,
    fin_send,
    fin_recv,
    xf_send,
    xf_recv,
    core_send,
    core_recv,
    z1_send,
    z1_recv,
    z2_send,
    z2_recv,
    go_sem,
    token_sem,
):
    s = lax.axis_index("section")
    t = lax.axis_index("tensor")
    d = lax.axis_index("dp")
    z, core = d // 2, d % 2
    n_z = n_dp // 2
    n_far = n_z // NEAR
    zi, zg = z % NEAR, z // NEAR
    shard, half_width = outs.shape[2:]
    small = shard // 2
    n_rows = q.shape[2]
    half_rows = n_rows // 2
    home = t // (n_tensor // 2)
    chunk = grad_ref.shape[1]
    first = s == 1

    n_x = n_tensor // 2
    ty, tx = t // n_x, lax.rem(t, n_x)

    def tensor_peer(j):
        return (ty + j // n_x) % 2 * n_x + (tx + j % n_x) % n_x

    def distance(j):
        return 2 * (j // n_x) + min(j % n_x, n_x - j % n_x)

    others = sorted(range(1, n_tensor), key=lambda j: -distance(j))

    def near_peer(j):
        return (zg * NEAR + lax.rem(zi + j, NEAR)) * 2 + core

    def far_peer(j):
        return (lax.rem(zg + j, n_far) * NEAR + zi) * 2 + core

    barrier = pltpu.get_barrier_semaphore()

    def hello(device):
        pl.semaphore_signal(barrier, inc=1, device_id=device, device_id_type=MESH)

    for j in range(1, n_tensor):
        hello({"tensor": tensor_peer(j)})
    for j in range(n_tensor):
        hello({"section": 1 - s, "tensor": tensor_peer(j)})
    hello({"dp": z * 2 + 1 - core})
    for j in range(1, NEAR):
        hello({"dp": near_peer(j)})
    for j in (1, n_far - 1):
        hello({"dp": far_peer(j)})

    loads = [
        pltpu.make_async_copy(src, dst, load_sem.at[i])
        for i, (src, dst) in enumerate(
            [
                (cot_hbm, cot),
                (xin_hbm, xin),
                (wo_hbm, wo),
                (q_hbm, q),
                (kv_hbm, kv),
                (wq_hbm, wq),
                (wkv_hbm, wkv),
                (gain_hbm, gain),
                (xn_hbm, xn),
            ]
        )
    ]
    for load in loads:
        load.start()

    loads[0].wait()
    for b in range(2):
        cot_folded[b] = folded(cot[...].astype(F32)[b * small : (b + 1) * small]).astype(BF16)
    loads[1].wait()
    for i in range(4):
        rows = xin[i // 2, i % 2].astype(F32)
        for b in range(2):
            xf_out[b, i] = folded(rows[b * small : (b + 1) * small]).astype(BF16)

    pl.semaphore_wait(barrier, 2 * n_tensor - 1 + 1 + NEAR - 1 + 2)

    def rows_of(index):
        return pl.ds(pl.multiple_of(index * shard, shard), shard)

    def block_of(b):
        return 2 * lax.rem(t, n_tensor // 2) + b

    def start_copy(item, b, j, section):
        return pltpu.make_async_remote_copy(
            src_ref=cot_folded.at[b],
            dst_ref=gathered.at[item, home, rows_of(block_of(b))],
            send_sem=ag_send.at[b, j],
            recv_sem=ag_recv.at[item, home, block_of(b)],
            device_id={"section": section, "tensor": tensor_peer(j)},
            device_id_type=MESH,
        )

    def own_shard_copy(b):
        return pltpu.make_async_copy(
            cot_folded.at[b],
            gathered.at[0, home, rows_of(block_of(b))],
            ag_recv.at[0, home, block_of(b)],
        )

    def reply_copy(k, h, item, j):
        return pltpu.make_async_remote_copy(
            src_ref=outs.at[k, h],
            dst_ref=gathered.at[item, h, rows_of(t)],
            send_sem=out_send.at[k, h, j],
            recv_sem=ag_recv.at[item, h, t],
            device_id={"section": 1 - s, "tensor": lax.rem(t + j, n_tensor)},
            device_id_type=MESH,
        )

    def arrival(k, h, r):
        return pltpu.make_async_remote_copy(
            src_ref=outs.at[0, h],
            dst_ref=gathered.at[k, h, r * shard : (r + 1) * shard],
            send_sem=out_send.at[0, h, 0],
            recv_sem=ag_recv.at[k, h, r],
            device_id={"section": 1 - s},
            device_id_type=MESH,
        )

    def reduce_copy(k, h, j):
        return pltpu.make_async_remote_copy(
            src_ref=parts.at[k, h, rows_of(tensor_peer(j))],
            dst_ref=landed.at[k, h, rows_of(j)],
            send_sem=rs_send.at[k, h, j],
            recv_sem=rs_recv.at[k, h, j],
            device_id={"tensor": tensor_peer(j)},
            device_id_type=MESH,
        )

    def result_owner(h):
        return h * (n_tensor // 2) + t // 2

    def final_copy(k, h, section):
        return pltpu.make_async_remote_copy(
            src_ref=outs.at[k, h],
            dst_ref=final.at[t % 2],
            send_sem=fin_send.at[h],
            recv_sem=fin_recv.at[t % 2],
            device_id={"section": section, "tensor": result_owner(h)},
            device_id_type=MESH,
        )

    def final_last(h):
        return pltpu.make_async_remote_copy(
            src_ref=outs.at[3, h],
            dst_ref=final.at[t % 2],
            send_sem=fin_send.at[2 + h],
            recv_sem=fin_recv.at[t % 2],
            device_id={"tensor": result_owner(h)},
            device_id_type=MESH,
        )

    def final_own(k, h):
        return pltpu.make_async_copy(outs.at[k, h], final.at[t % 2], fin_recv.at[t % 2])

    def final_arrival(b):
        return pltpu.make_async_remote_copy(
            src_ref=outs.at[0, 0],
            dst_ref=final.at[b],
            send_sem=fin_send.at[0],
            recv_sem=fin_recv.at[b],
            device_id={"section": 1 - s},
            device_id_type=MESH,
        )

    def input_copy(b):
        return pltpu.make_async_remote_copy(
            src_ref=xf_out.at[b],
            dst_ref=xf.at[home],
            send_sem=xf_send.at[b],
            recv_sem=xf_recv.at[home],
            device_id={"tensor": block_of(b)},
            device_id_type=MESH,
        )

    def input_own(b):
        return pltpu.make_async_copy(xf_out.at[b], xf.at[home], xf_recv.at[home])

    def input_arrival(h):
        return pltpu.make_async_remote_copy(
            src_ref=xf_out.at[0],
            dst_ref=xf.at[h],
            send_sem=xf_send.at[0],
            recv_sem=xf_recv.at[h],
            device_id={"section": 1 - s},
            device_id_type=MESH,
        )

    def core_copy(slot):
        return pltpu.make_async_remote_copy(
            src_ref=core_out.at[slot],
            dst_ref=core_in.at[slot],
            send_sem=core_send.at[slot],
            recv_sem=core_recv.at[slot],
            device_id={"dp": z * 2 + 1 - core},
            device_id_type=MESH,
        )

    def near_copy(slot, part, j):
        span = pl.ds(part * (n_far // 2), n_far // 2)
        return pltpu.make_async_remote_copy(
            src_ref=z1_out.at[slot, lax.rem(zi + j, NEAR), span],
            dst_ref=z1_in.at[slot, j, span],
            send_sem=z1_send.at[slot, part, j],
            recv_sem=z1_recv.at[slot, part, j],
            device_id={"dp": near_peer(j)},
            device_id_type=MESH,
        )

    def far_copy(slot, j):
        return pltpu.make_async_remote_copy(
            src_ref=z2_out.at[slot, j],
            dst_ref=z2_in.at[slot, j],
            send_sem=z2_send.at[slot, j],
            recv_sem=z2_recv.at[slot, j],
            device_id={"dp": far_peer(j)},
            device_id_type=MESH,
        )

    def greet(round_index):
        for j in (1, n_far - 1):
            pl.semaphore_signal(
                token_sem.at[round_index],
                inc=1,
                device_id={"dp": far_peer(j)},
                device_id_type=MESH,
            )

    def greeted(round_index):
        pl.semaphore_wait(token_sem.at[round_index], 2)

    def turn(slot):
        def block(b, carry):
            columns = pl.ds(pl.multiple_of(b * 128, 128), 128)
            for place in range(2):
                flat = xn[slot, 1 - place, :, columns].T
                for i in range(128 // chunk):
                    owner = b * (128 // chunk) + i
                    oz, oc = owner // 2, owner % 2
                    where = (oz % NEAR) * n_far + oz // NEAR
                    turned[
                        slot,
                        oc,
                        pl.ds(pl.multiple_of(where * chunk, chunk), chunk),
                        place * n_rows : (place + 1) * n_rows,
                    ] = flat[i * chunk : (i + 1) * chunk]
            return carry

        lax.fori_loop(0, xn.shape[3] // 128, block, 0)

    def gradient(slot):
        rows = dkv[slot]

        def theirs(b, carry):
            span = pl.ds(pl.multiple_of(b * 256, 256), 256)
            core_out[slot, span] = dot(turned[slot, 1 - core, span], rows, NN).astype(BF16)
            return carry

        def ours(b, carry):
            span = pl.ds(pl.multiple_of(b * 256, 256), 256)
            core_own[slot, span] = dot(turned[slot, core, span], rows, NN)
            return carry

        count = core_out.shape[1] // 256
        lax.fori_loop(0, count, theirs, 0)
        core_copy(slot).start()
        lax.fori_loop(0, count, ours, 0)

    far_order = [(i + n_far // 4) % n_far for i in range(n_far)]

    def sum_rows(i, j):
        where = (i * n_far + lax.rem(zg + j, n_far)) * chunk
        return pl.ds(pl.multiple_of(where, chunk), chunk)

    def near_phase(slot):
        core_copy(slot).wait_recv()
        for part in range(2):
            for i in range(NEAR):
                for place in range(part * (n_far // 2), (part + 1) * (n_far // 2)):
                    span = sum_rows(i, far_order[place])
                    total = core_own[slot, span] + core_in[slot, span].astype(F32)
                    core_own[slot, span] = total
                    z1_out[slot, i, place] = total.astype(BF16)
            for j in range(1, NEAR):
                near_copy(slot, part, j).start()

    def far_phase(slot, part):
        for j in range(1, NEAR):
            near_copy(slot, part, j).wait_recv()
        places = range(part * (n_far // 2), (part + 1) * (n_far // 2))
        for place in sorted(places, key=lambda p: abs(far_order[p] - n_far // 2)):
            j = far_order[place]
            total = core_own[slot, sum_rows(zi, j)]
            for i in range(1, NEAR):
                total = total + z1_in[slot, i, place].astype(F32)
            if j:
                z2_out[slot, j] = total.astype(BF16)
                far_copy(slot, j).start()
            else:
                grad_ref[slot] = total

    def last_phase(slot):
        total = grad_ref[slot]
        for j in range(1, n_far):
            far_copy(slot, j).wait_recv()
            total = total + z2_in[slot, j].astype(F32)
        grad_ref[slot] = total

    @pl.when(first)
    def _():
        for b in range(2):
            own_shard_copy(b).start()
        for j in others:
            for b in range(2):
                start_copy(0, b, j, s).start()

    for b in range(2):

        @pl.when(block_of(b) != t)
        def _():
            input_copy(b).start()

        @pl.when(block_of(b) == t)
        def _():
            input_own(b).start()

    greet(0)
    for load in loads[2:]:
        load.wait()
    turn(1)

    @pl.when(jnp.logical_not(first))
    def _():
        pl.semaphore_wait(go_sem, 1)
        for j in range(n_tensor):
            for b in range(2):
                start_copy(1, b, j, 1 - s).start()

    def norm_half(k, h, slot, micro):
        x = xf[h, slot * 2 + micro].astype(F32)

        def over_rows(values):
            sums = jnp.sum(values, axis=-1, keepdims=True)
            mean = (sums[:small] + sums[small:]) / (2 * half_width)
            return jnp.concatenate([mean, mean], axis=0)

        r = lax.rsqrt(over_rows(x * x) + 1e-05)
        d_normed = parts[k, h, rows_of(t)].astype(F32)
        for j in range(1, n_tensor):
            reduce_copy(k, h, j).wait_recv()
            d_normed = d_normed + landed[k, h, j * shard : (j + 1) * shard].astype(F32)
        row = gain[slot]
        gains = jnp.concatenate(
            [
                jnp.broadcast_to(row[:, :half_width], (small, half_width)),
                jnp.broadcast_to(row[:, half_width:], (small, half_width)),
            ],
            axis=0,
        )
        scaled = d_normed * gains
        d_input = r * scaled - x * (r * r * r * over_rows(x * scaled))
        outs[k, h] = (gathered[k, h, rows_of(t)].astype(F32) + d_input).astype(BF16)

        @pl.when(first)
        def _():
            for j in range(n_tensor):
                reply_copy(k, h, k, j).start()

        @pl.when(jnp.logical_and(jnp.logical_not(first), k < 2))
        def _():
            for j in range(n_tensor):
                reply_copy(k, h, k + 2, j).start()

        @pl.when(jnp.logical_and(jnp.logical_not(first), k == 2))
        def _():
            final_copy(k, h, 1 - s).start()

        @pl.when(jnp.logical_and(jnp.logical_not(first), k == 3))
        def _():
            @pl.when(result_owner(h) != t)
            def _():
                final_last(h).start()

            @pl.when(result_owner(h) == t)
            def _():
                final_own(k, h).start()

    def kv_rows(h, place):
        start = place * n_rows + h * half_rows
        return pl.ds(pl.multiple_of(start, half_rows), half_rows)

    def project(k, h, slot, place):
        d_query, d_keyval = kept[h], dkv[slot, kv_rows(h, place)]
        tile = half_width // 2
        for c in range(2):
            sides = []
            for side in range(2):
                span = slice(side * half_width + c * tile, side * half_width + (c + 1) * tile)
                sides.append(dot(d_query, wq[slot, span], NT) + dot(d_keyval, wkv[slot, span], NT))
            blocks = []
            for r in range(n_tensor):
                blocks += [side[r * small : (r + 1) * small] for side in sides]
            parts[k, h, :, c * tile : (c + 1) * tile] = jnp.concatenate(blocks, axis=0).astype(BF16)
        for far, near in zip(others, reversed(others)):
            reduce_copy(k, h, far * (1 - core) + near * core).start()

    def prepare(k):
        slot, micro = 1 - k // 2, 1 - k % 2
        for h in range(2):
            base = h * half_rows
            shares[h, : 2 * (base + half_rows)] = attention_shares(
                q[slot, micro, base : base + half_rows], kv[slot, micro, : base + half_rows], base
            )

    def step(k, carry):
        slot = 1 - k // 2
        place = k % 2
        micro = 1 - place
        tail = jnp.logical_and(k == 3, jnp.logical_not(first))
        for h in (1, 0):
            for r in range(n_tensor):
                arrival(k, h, r).wait_recv()
            low = dot(gathered[k, h], wo[slot, :, :half_width], NT)
            high = dot(gathered[k, h], wo[slot, :, half_width:], NT)
            d_attn = jnp.concatenate(
                [
                    low[r * shard : r * shard + small] + high[r * shard + small : (r + 1) * shard]
                    for r in range(n_tensor)
                ],
                axis=0,
            ).astype(BF16)
            base = h * half_rows
            d_query, d_keyval = attention_grads(
                q[slot, micro, base : base + half_rows],
                kv[slot, micro, : base + half_rows],
                d_attn,
                shares[h, : 2 * (base + half_rows)],
            )
            if h:
                carried[...] = d_keyval[:half_rows]
                d_keyval = d_keyval[half_rows:].astype(BF16)
            else:
                d_keyval = (d_keyval + carried[...]).astype(BF16)
            dkv[slot, kv_rows(h, place)] = d_keyval
            kept[h] = d_query
            if h:

                @pl.when(jnp.logical_not(tail))
                def _():
                    project(k, 1, slot, place)

            else:

                @pl.when(tail)
                def _():
                    gradient(0)
                    project(k, 1, slot, place)

                project(k, 0, slot, place)

                @pl.when(tail)
                def _():
                    near_phase(0)

        @pl.when(jnp.logical_and(first, k == 0))
        def _():
            pl.semaphore_signal(go_sem, inc=1, device_id={"section": 1 - s}, device_id_type=MESH)

        @pl.when(k == 0)
        def _():
            turn(0)
            for h in range(2):
                input_arrival(h).wait_recv()

        @pl.when(jnp.logical_and(place == 1, jnp.logical_not(tail)))
        def _():
            gradient(slot)

        @pl.when(k < 2)
        def _():
            greeted(k)
            greet(k + 1)

        @pl.when(k < 3)
        def _():
            prepare(k + 1)

        @pl.when(tail)
        def _():
            far_phase(0, 0)

        norm_half(k, 1, slot, micro)

        @pl.when(tail)
        def _():
            far_phase(0, 1)

        norm_half(k, 0, slot, micro)

        @pl.when(jnp.logical_and(place == 1, jnp.logical_not(tail)))
        def _():
            near_phase(slot)

        @pl.when(k == 2)
        def _():
            greeted(2)
            far_phase(1, 0)
            far_phase(1, 1)

        return carry

    prepare(0)
    lax.fori_loop(0, 4, step, 0)

    @pl.when(first)
    def _():
        far_phase(0, 0)
        far_phase(0, 1)

    for b in range(2):
        final_arrival(b).wait_recv()
    out_ref[...] = jnp.concatenate(
        [unfolded(final[b].astype(F32)) for b in range(2)], axis=0
    ).astype(BF16)

    @pl.when(first)
    def _():
        for j in range(1, n_tensor):
            for b in range(2):
                start_copy(0, b, j, s).wait_send()
        for k in range(4):
            for h in range(2):
                for j in range(n_tensor):
                    reply_copy(k, h, k, j).wait_send()

    @pl.when(jnp.logical_not(first))
    def _():
        for j in range(n_tensor):
            for b in range(2):
                start_copy(1, b, j, 1 - s).wait_send()
        for k in range(2):
            for h in range(2):
                for j in range(n_tensor):
                    reply_copy(k, h, k + 2, j).wait_send()
        for h in range(2):
            final_copy(2, h, 1 - s).wait_send()

            @pl.when(result_owner(h) != t)
            def _():
                final_last(h).wait_send()

    for b in range(2):

        @pl.when(block_of(b) != t)
        def _():
            input_copy(b).wait_send()

    last_phase(1)
    last_phase(0)
    for k in range(4):
        for h in range(2):
            for j in range(1, n_tensor):
                reduce_copy(k, h, j).wait_send()
    for slot in range(2):
        core_copy(slot).wait_send()
        for part in range(2):
            for j in range(1, NEAR):
                near_copy(slot, part, j).wait_send()
        for j in range(1, n_far):
            far_copy(slot, j).wait_send()


def on_device(
    n_tensor,
    n_dp,
    cotangent,
    saved_input,
    saved_normed,
    saved_query,
    saved_keyval,
    norm_gain,
    w_query,
    w_keyval,
    w_output,
):
    layers, _, micros, _, shard, width = saved_input.shape
    n_rows, q_width = saved_query.shape[4:]
    kv_width = w_keyval.shape[4]
    chunk = width // n_dp
    n_z = n_dp // 2
    n_far = n_z // NEAR
    items = layers * micros
    any_spec = pl.BlockSpec(memory_space=pl.ANY)
    vmem_spec = pl.BlockSpec(memory_space=pltpu.VMEM)
    dma = pltpu.SemaphoreType.DMA
    input_grad, keyval_grad = pl.pallas_call(
        functools.partial(kernel, n_tensor, n_dp),
        out_shape=(
            jax.ShapeDtypeStruct((shard, width), BF16),
            jax.ShapeDtypeStruct((layers, chunk, kv_width), F32),
        ),
        in_specs=[any_spec] * 9,
        out_specs=(vmem_spec, vmem_spec),
        scratch_shapes=[
            pltpu.VMEM((layers, micros, shard, width), BF16),
            pltpu.VMEM((layers, micros, n_rows, width), BF16),
            pltpu.VMEM((layers, micros, n_rows, q_width), BF16),
            pltpu.VMEM((layers, micros, n_rows, kv_width), BF16),
            pltpu.VMEM((layers, 1, width), F32),
            pltpu.VMEM((layers, width, q_width), BF16),
            pltpu.VMEM((layers, width, kv_width), BF16),
            pltpu.VMEM((layers, q_width, width), BF16),
            pltpu.VMEM((items, 2, n_rows, width // 2), BF16),
            pltpu.VMEM((items, 2, n_rows, width // 2), BF16),
            pltpu.VMEM((items, 2, n_rows, width // 2), BF16),
            pltpu.VMEM((items, 2, shard, width // 2), BF16),
            pltpu.VMEM((2, shard, width // 2), BF16),
            pltpu.VMEM((shard, width), BF16),
            pltpu.VMEM((2, shard, width // 2), BF16),
            pltpu.VMEM((2, items, shard, width // 2), BF16),
            pltpu.VMEM((2, items, shard, width // 2), BF16),
            pltpu.VMEM((n_rows // 2, kv_width), F32),
            pltpu.VMEM((2, n_rows // 2, q_width), BF16),
            pltpu.VMEM((2, 2 * n_rows, q_width // 2), F32),
            pltpu.VMEM((layers, micros * n_rows, kv_width), BF16),
            pltpu.VMEM((layers, 2, width // 2, micros * n_rows), BF16),
            pltpu.VMEM((layers, width // 2, kv_width), BF16),
            pltpu.VMEM((layers, width // 2, kv_width), F32),
            pltpu.VMEM((layers, width // 2, kv_width), BF16),
            pltpu.VMEM((layers, NEAR, n_far, chunk, kv_width), BF16),
            pltpu.VMEM((layers, NEAR, n_far, chunk, kv_width), BF16),
            pltpu.VMEM((layers, n_far, chunk, kv_width), BF16),
            pltpu.VMEM((layers, n_far, chunk, kv_width), BF16),
            dma((9,)),
            dma((2, n_tensor)),
            dma((items, 2, n_tensor)),
            dma((items, 2, n_tensor)),
            dma((items, 2, n_tensor)),
            dma((items, 2, n_tensor)),
            dma((4,)),
            dma((2,)),
            dma((2,)),
            dma((2,)),
            dma((layers,)),
            dma((layers,)),
            dma((layers, 2, NEAR)),
            dma((layers, 2, NEAR)),
            dma((layers, n_far)),
            dma((layers, n_far)),
            pltpu.SemaphoreType.REGULAR,
            pltpu.SemaphoreType.REGULAR((3,)),
        ],
        compiler_params=pltpu.CompilerParams(
            collective_id=0, has_side_effects=True, vmem_limit_bytes=56 * 2**20
        ),
        name="backward",
    )(
        cotangent.reshape(shard, width),
        saved_input.reshape(layers, micros, shard, width),
        saved_normed.reshape(layers, micros, n_rows, width),
        saved_query.reshape(layers, micros, n_rows, q_width),
        saved_keyval.reshape(layers, micros, n_rows, kv_width),
        norm_gain,
        w_query.reshape(layers, width, q_width),
        w_keyval.reshape(layers, width, kv_width),
        w_output.reshape(layers, q_width, width),
    )
    return (
        input_grad[None, None],
        keyval_grad.reshape(layers, 1, chunk, 1, kv_width),
    )


def solution(mesh):
    in_specs = (
        P("section", "dp", "tensor", None),
        P(None, "section", None, "dp", "tensor", None),
        P(None, "section", None, "dp", None, None),
        P(None, "section", None, "dp", None, "tensor"),
        P(None, "section", None, "dp", None, "tensor", None),
        P(None, "section", None),
        P(None, "section", None, "tensor"),
        P(None, "section", None, "tensor", None),
        P(None, "section", "tensor", None),
    )
    out_specs = (P("section", "dp", "tensor", None), P(None, "section", "dp", "tensor", None))
    return jax.shard_map(
        functools.partial(on_device, mesh.shape["tensor"], mesh.shape["dp"]),
        mesh=mesh,
        in_specs=in_specs,
        out_specs=out_specs,
        check_vma=False,
    )
```
